32 devices in a mesh: row: 4 (over x, core), col: 8 (over z, y).
Axes of the slice: x: 2, y: 2, z: 4, core: 2. Of those that a mesh axis runs over, the one named last changes fastest.
Arguments:
- upper_blocks: float32 [32, 9, 128, 128], P(('row', 'col')), as said below
- members: int32 [32, 9], P(('row', 'col')), may hold values from -1 to 31, as said below
Outputs:
- purified_blocks: float32 [32, 9, 128, 128], P(('row', 'col'))
The draws below stay inside these ranges and needn't reach their ends.
Inputs may be any that keep to these rules, and one draw needn't show every extreme that they name: `members`: write j = r * 8 + q. Slot 0 holds j; slots 1 to 4 hold the blocks r * 8 + (q + d) mod 8 for d = -1, 1, -2, 2 in that order; slot 5 holds the block for d equal to half of 8; slot 6 the block for d = 3 when q is even and d = -3 when q is odd; slots 3 to 6 may hold -1 for an absent block; slots 7 and 8 hold blocks p * 8 + q of two other values p. The pattern is symmetric: a lists b exactly when b lists a (slots 1 and 2, and 3 and 4, trade places; slots 5 and 6 keep theirs; slots 7 and 8 trade places), and the blocks of slots 7 and 8 of one column never list each other. Slots 0, 1, 2, 7 and 8 are always present, and some block column has all 9. Slot t of upper_blocks[j] holds the block in block row members[j, t] and block column j when members[j, t] >= 0 and members[j, t] <= j, and zeros otherwise; the slot 0 block is symmetric.
All inputs are finite; a program needn't handle non-finite values.
Results may differ from the reference program's by a relative error of at most 0.0003.
Values sent between devices are 32-bit elements; how exact they have to be, the bound alone decides.
No kernel may reach another device: no remote copies, remote signals or barrier semaphores. Data moves between devices by JAX's collectives and lax.ppermute only.
A program may use at most 128 MiB of HBM per device.

```python
import jax
import jax.numpy as jnp
from jax import lax

BS = 128
KMAX = 9
PURIFY = 3
GROUP_ROWS = 4
GROUP_COLS = 8
NB = 32


def link_pattern(key):
    base = jax.random.fold_in(key, 7001)
    half_cols = GROUP_COLS // 2
    subkeys = jax.random.split(jax.random.fold_in(base, 1), GROUP_COLS)
    orders = jax.vmap(lambda subkey: jax.random.permutation(subkey, GROUP_ROWS))(subkeys).astype(jnp.int32)
    places = jnp.argsort(orders, axis=1).astype(jnp.int32)
    far_two = jax.random.randint(jax.random.fold_in(base, 2), (GROUP_ROWS, GROUP_COLS), 0, 2)
    far_three = jax.random.randint(jax.random.fold_in(base, 3), (GROUP_ROWS, GROUP_COLS), 0, 2)
    far_half = jax.random.randint(jax.random.fold_in(base, 4), (GROUP_ROWS, half_cols), 0, 2)
    far_two = far_two.at[0, 0].set(1).at[0, GROUP_COLS - 2].set(1)
    far_three = far_three.at[0, 0].set(1)
    far_half = far_half.at[0, 0].set(1)
    row_grid = jnp.broadcast_to(jnp.arange(GROUP_ROWS, dtype=jnp.int32)[:, None], (GROUP_ROWS, GROUP_COLS))
    col_grid = jnp.broadcast_to(jnp.arange(GROUP_COLS, dtype=jnp.int32)[None, :], (GROUP_ROWS, GROUP_COLS))

    def block_at(row_part, col_part):
        return row_part * GROUP_COLS + jnp.mod(col_part, GROUP_COLS)
    left_two = jnp.where(far_two[row_grid, jnp.mod(col_grid - 2, GROUP_COLS)] == 1, block_at(row_grid, col_grid - 2), -1)
    right_two = jnp.where(far_two == 1, block_at(row_grid, col_grid + 2), -1)
    half_slot = jnp.where(far_half[row_grid, jnp.mod(col_grid, half_cols)] == 1, block_at(row_grid, col_grid + half_cols), -1)
    even_col = jnp.mod(col_grid, 2) == 0
    three_flag = jnp.where(even_col, far_three[row_grid, col_grid], far_three[row_grid, jnp.mod(col_grid - 3, GROUP_COLS)])
    three_slot = jnp.where(three_flag == 1, block_at(row_grid, jnp.where(even_col, col_grid + 3, col_grid - 3)), -1)
    place = places[col_grid, row_grid]
    before = orders[col_grid, jnp.mod(place - 1, GROUP_ROWS)]
    after = orders[col_grid, jnp.mod(place + 1, GROUP_ROWS)]
    listed = jnp.stack([block_at(row_grid, col_grid), block_at(row_grid, col_grid - 1), block_at(row_grid, col_grid + 1), left_two, right_two, half_slot, three_slot, block_at(before, col_grid), block_at(after, col_grid)], axis=-1)
    return listed.reshape(NB, KMAX).astype(jnp.int32)


def draw_members(key, part):
    return link_pattern(key)


def draw_upper_blocks(key, part):
    listed = link_pattern(key)
    values = jax.random.uniform(jax.random.fold_in(key, 7002), (NB, KMAX, BS, BS), jnp.float32, -0.01, 0.01)
    diagonal = jax.random.uniform(jax.random.fold_in(key, 7003), (NB, BS), jnp.float32, 0.15, 0.85)
    identity = jnp.eye(BS, dtype=jnp.float32)
    first = values[:, 0]
    symmetric = 0.5 * (first + jnp.transpose(first, (0, 2, 1)))
    symmetric = symmetric * (1.0 - identity)[None] + diagonal[:, :, None] * identity[None]
    values = values.at[:, 0].set(symmetric)
    keep_mask = ((listed >= 0) & (listed <= jnp.arange(NB, dtype=jnp.int32)[:, None])).astype(jnp.float32)
    return values * keep_mask[:, :, None, None]


def setup_inputs(seed: int = 0) -> dict:
    keys = jax.random.split(jax.random.key(seed), 3)
    upper_blocks = draw_upper_blocks(jax.random.fold_in(keys[2], 71), 0)
    members = draw_members(jax.random.fold_in(keys[2], 71), 0)
    return dict(upper_blocks=upper_blocks, members=members)


highest = lax.Precision.HIGHEST


def assemble(own_list, member_cols, member_lists):
    slot_count = own_list.shape[0]
    block_width = member_cols.shape[-1]
    matches = ((member_lists[:, :, None] == own_list[None, None, :]) & (own_list >= 0)[None, None, :]).astype(jnp.float32)
    upper_part = jnp.einsum("uts,utxy->suxy", matches, member_cols, precision=highest)
    off_diagonal = (1.0 - jnp.eye(slot_count, dtype=jnp.float32))[:, :, None, None]
    full_blocks = upper_part + jnp.transpose(upper_part, (1, 0, 3, 2)) * off_diagonal
    order_total = slot_count * block_width
    return jnp.transpose(full_blocks, (0, 2, 1, 3)).reshape(order_total, order_total)


def polynomial_columns(submatrix, block_width):
    first_cols = submatrix[:, :block_width]
    square_cols = jnp.dot(submatrix, first_cols, precision=highest, preferred_element_type=jnp.float32)
    cube_cols = jnp.dot(submatrix, square_cols, precision=highest, preferred_element_type=jnp.float32)
    return first_cols, square_cols, cube_cols


def purify(blocks, members):
    block_width = blocks.shape[-1]

    def column_terms(column_index):
        own_list = members[column_index]
        safe_index = jnp.maximum(own_list, 0)
        present = (own_list >= 0).astype(jnp.float32)
        member_cols = blocks[safe_index] * present[:, None, None, None]
        member_lists = members[safe_index]
        return polynomial_columns(assemble(own_list, member_cols, member_lists), block_width)

    first_cols, square_cols, cube_cols = lax.map(column_terms, jnp.arange(NB, dtype=jnp.int32))
    low_trace = jnp.sum(jnp.diagonal(first_cols[:, :block_width] - square_cols[:, :block_width], axis1=1, axis2=2))
    high_trace = jnp.sum(jnp.diagonal(square_cols[:, :block_width] - cube_cols[:, :block_width], axis1=1, axis2=2))
    purity_coef = high_trace / low_trace
    columns = ((1.0 - 2.0 * purity_coef) * first_cols + (1.0 + purity_coef) * square_cols - cube_cols) / (1.0 - purity_coef)
    keep_mask = ((members >= 0) & (members <= jnp.arange(NB, dtype=jnp.int32)[:, None])).astype(jnp.float32)
    return columns.reshape(NB, KMAX, block_width, block_width) * keep_mask[:, :, None, None]


def reference(upper_blocks, members):
    blocks = upper_blocks
    for repeat in range(PURIFY):
        blocks = purify(blocks, members)
    return blocks
```

```python
import functools
import math

import jax
import jax.numpy as jnp
from jax import lax
from jax.experimental import pallas as pl
from jax.experimental.pallas import tpu as pltpu
from jax.sharding import PartitionSpec as P

PURIFY = 3
BW = 128
TILE = 256
NEAR = 7
PACK = BW + 8
SPARE = 8 * 1024 * 1024
MOST = 60 * 1024 * 1024

f32 = jnp.float32
bf16 = jnp.bfloat16


def offsets(q, nq):
    return [0, -1, 1, -2, 2, nq // 2, 3 if q % 2 == 0 else -3]


@functools.lru_cache
def pattern(nq):
    pairs = [(q, q) for q in range(nq)]
    for b in range(nq):
        for d in offsets(b, nq)[1:]:
            a = (b + d) % nq
            if a < b:
                pairs.append((a, b))
    return tuple(pairs)


@functools.lru_cache
def pair_index(nq):
    return {pair: i for i, pair in enumerate(pattern(nq))}


def slot_of(a, b, nq):
    return [(b + d) % nq for d in offsets(b, nq)].index(a)


@functools.lru_cache
def tiles(nq):
    index = pair_index(nq)
    n = nq * BW // TILE
    per = TILE // BW

    def live(i, j):
        lo, hi = min(i, j), max(i, j)
        return any(
            (a, b) in index or (b, a) in index
            for a in range(lo * per, (lo + 1) * per)
            for b in range(hi * per, (hi + 1) * per)
        )

    out = []
    for i in range(n):
        for j in range(i, n):
            if live(i, j):
                inner = [k for k in range(n) if live(i, k) and live(k, j)]
                out.append((i, j, inner))
    return out


def split(x):
    hi = x.astype(bf16)
    return hi, (x - hi.astype(f32)).astype(bf16)


def mm(a, b):
    return jnp.dot(a, b, preferred_element_type=f32)


def dot3(ah, al, bh, bl):
    return mm(ah, bh) + (mm(ah, bl) + mm(al, bh))


def dotf(a, b):
    return dot3(*split(a), *split(b))


def row_col():
    return (
        lax.broadcasted_iota(jnp.int32, (BW, BW), 0),
        lax.broadcasted_iota(jnp.int32, (BW, BW), 1),
    )


def total(x):
    s = jnp.sum(jnp.sum(x, axis=0, keepdims=True), axis=1, keepdims=True)
    return jnp.broadcast_to(s, (1, BW))


def pack_pair(ref, first, second):
    i, j = row_col()
    ref[0:BW, :] = jnp.where(i <= j, first, second)
    ref[BW : BW + 1, :] = jnp.sum(jnp.where(i == j, second, 0.0), axis=0, keepdims=True)


def unpack_pair(block, diagonal):
    i, j = row_col()
    flipped = block.T
    first = jnp.where(i <= j, block, flipped)
    second = jnp.where(i > j, block, jnp.where(i == j, diagonal, flipped))
    return first, second


def at(q):
    return pl.ds(pl.multiple_of(q * BW, BW), BW)


def cut(q):
    return slice(q * BW, (q + 1) * BW)


def put_dense(hi_ref, lo_ref, a, b, block):
    hi, lo = split(block)
    hi_ref[cut(a), cut(b)] = hi
    lo_ref[cut(a), cut(b)] = lo
    if a != b:
        hi, lo = split(block.T)
        hi_ref[cut(b), cut(a)] = hi
        lo_ref[cut(b), cut(a)] = lo


def clear_unlinked(hi_ref, lo_ref, nq):
    index = pair_index(nq)
    zero = jnp.zeros((BW, BW), bf16)
    for a in range(nq):
        for b in range(nq):
            if (min(a, b), max(a, b)) not in index:
                hi_ref[cut(a), cut(b)] = zero
                lo_ref[cut(a), cut(b)] = zero


def tile_products(ah, al, bh, bl, nq):
    index = pair_index(nq)
    per = TILE // BW
    n = nq * BW // TILE
    for i, j, inner in tiles(nq):
        rows, cols = slice(i * TILE, (i + 1) * TILE), slice(j * TILE, (j + 1) * TILE)
        if len(inner) == n:
            acc = dot3(ah[rows, :], al[rows, :], bh[:, cols], bl[:, cols])
        else:
            acc = None
            for k in inner:
                mid = slice(k * TILE, (k + 1) * TILE)
                part = dot3(ah[rows, mid], al[rows, mid], bh[mid, cols], bl[mid, cols])
                acc = part if acc is None else acc + part
        for x in range(per):
            for y in range(per):
                a, b = i * per + x, j * per + y
                if (a, b) in index:
                    yield (a, b), acc[cut(x), cut(y)]


def square_part(nq, q, own_pack, m_ref, mh, ml, link, s_ref, sh, sl, out_ref):
    index = pair_index(nq)
    clear_unlinked(sh, sl, nq)
    trace = jnp.zeros((BW, BW), f32)
    norm = jnp.zeros((BW, BW), f32)
    inner = jnp.zeros((BW, BW), f32)
    i, j = row_col()
    for (a, b), block in tile_products(mh, ml, mh, ml, nq):
        if a != b:
            block = block * link[a : a + 1, cut(b)]
        at_list = index[(a, b)]
        s_ref[at_list] = block
        put_dense(sh, sl, a, b, block)
        own = m_ref[at_list]
        if a == b:
            trace = trace + own
            norm = norm + own * own
            inner = inner + own * block
        else:
            norm = norm + 2.0 * (own * own)
            inner = inner + 2.0 * (own * block)
    g, e = unpack_pair(own_pack[0:BW, :], own_pack[BW : BW + 1, :])
    d = m_ref[q]
    dg = dotf(d, g)
    s0 = s_ref[q] + g
    k0 = dot3(mh[at(q), :], ml[at(q), :], sh[:, at(q)], sl[:, at(q)]) + (dg + dg.T) + e
    pack_pair(out_ref, s0, k0)
    out_ref[BW + 1 : BW + 2, :] = total(jnp.where(i == j, trace, 0.0))
    out_ref[BW + 2 : BW + 3, :] = total(norm)
    out_ref[BW + 3 : BW + 4, :] = total(inner)
    out_ref[BW + 4 : BW + 8, :] = jnp.zeros((4, BW), f32)


def first_kernel(nq, ids, near, own_pack, m_ref, mh, ml, link, s_ref, sh, sl, out_ref):
    q = ids[1]
    clear_unlinked(mh, ml, nq)
    link[...] = jnp.zeros_like(link)
    for (a, b), place in pair_index(nq).items():
        t = slot_of(a, b, nq)
        block = near[b, cut(t), :]
        m_ref[place] = block
        put_dense(mh, ml, a, b, block)
    for a in range(nq):
        present = jnp.where(near[a, NEAR * BW : NEAR * BW + 1, :] >= 0.0, 1.0, 0.0)
        for t, d in enumerate(offsets(a, nq)):
            b = (a + d) % nq
            link[a : a + 1, cut(b)] = jnp.broadcast_to(present[:, t : t + 1], (1, BW))
    square_part(nq, q, own_pack, m_ref, mh, ml, link, s_ref, sh, sl, out_ref)


def assemble(nq, q, coef, packs, x_ref, y_ref, m_old, held, m_ref, mh, ml):
    index = pair_index(nq)
    c = coef[0:1, :]
    inv = coef[1:2, :]
    for k in range(nq):
        held[k ^ q] = packs[k][...]
    clear_unlinked(mh, ml, nq)
    for b in range(nq):
        g, e = unpack_pair(held[b, 0:BW, :], held[b, BW : BW + 1, :])
        gh, gl = split(g)
        for (a, b2), place in index.items():
            if b2 != b:
                continue
            fix = dot3(*split(m_old[place]), gh, gl)
            block = x_ref[place] + c * y_ref[place]
            if a == b:
                block = block + (1.0 + c) * g - (fix + fix.T + e)
            else:
                block = block - fix
            block = block * inv
            m_ref[place] = block
            put_dense(mh, ml, a, b, block)


def next_kernel(nq, ids, coef, *refs):
    packs, own_pack, refs = refs[:nq], refs[nq], refs[nq + 1 :]
    x_ref, y_ref, m_old, link, m_ref, mh, ml, s_ref, sh, sl, out_ref, held = refs
    q = ids[1]
    assemble(nq, q, coef, packs, x_ref, y_ref, m_old, held, m_ref, mh, ml)
    square_part(nq, q, own_pack, m_ref, mh, ml, link, s_ref, sh, sl, out_ref)


def cube_kernel(nq, m_ref, mh, ml, s_ref, sh, sl, link, x_ref, y_ref):
    index = pair_index(nq)
    for (a, b), block in tile_products(mh, ml, sh, sl, nq):
        if a != b:
            block = block * link[a : a + 1, cut(b)]
        place = index[(a, b)]
        m, s = m_ref[place], s_ref[place]
        x_ref[place] = (m + s) - block
        y_ref[place] = s - 2.0 * m


def edge_ends(lists, nq, e):
    far = lax.div(lists[e, 8], jnp.int32(nq))
    return jnp.minimum(far, e), jnp.maximum(far, e)


def cross_tail(nr, nq, ids, lists, d_ref, u_ref, su_ref, v_ref, pack_ref):
    r = ids[0]
    norm = jnp.zeros((BW, BW), f32)
    inner = jnp.zeros((BW, BW), f32)
    for e in range(nr):
        lo, hi = edge_ends(lists, nq, e)
        u = u_ref[e]
        uh, ul = split(u)
        dlo = split(d_ref[lo])
        su = dot3(uh, ul, *split(d_ref[hi])) + dot3(*dlo, uh, ul)
        su_ref[e] = su
        v_ref[e] = dot3(*dlo, *split(su))
        norm = norm + u * u
        inner = inner + u * su
    g_sum = jnp.zeros((BW, BW), f32)
    e_sum = jnp.zeros((BW, BW), f32)
    for slot in (7, 8):
        far = lax.div(lists[r, slot], jnp.int32(nq))
        u = u_ref[r if slot == 8 else far]
        flipped = u.T
        mine = r > far
        cu = split(jnp.where(mine, u, flipped))
        cut_ = split(jnp.where(mine, flipped, u))
        g_sum = g_sum + dot3(*cut_, *cu)
        t = dot3(*split(d_ref[far]), *cu)
        e_sum = e_sum + dot3(*cut_, *split(t))
    pack_pair(pack_ref, g_sum, e_sum)
    pack_ref[BW + 1 : BW + 2, :] = 2.0 * total(norm)
    pack_ref[BW + 2 : BW + 3, :] = 3.0 * total(inner)
    pack_ref[BW + 3 : BW + 8, :] = jnp.zeros((5, BW), f32)


def cross_first_kernel(nr, nq, ids, lists, row, d_ref, u_ref, su_ref, v_ref, pack_ref):
    for e in range(nr):
        d_ref[e] = row[e, cut(0), :]
    for e in range(nr):
        far = lax.div(lists[e, 8], jnp.int32(nq))
        here = row[e, cut(2), :]
        there = row[far, cut(1), :]
        u_ref[e] = jnp.where(far < e, here, there)
    cross_tail(nr, nq, ids, lists, d_ref, u_ref, su_ref, v_ref, pack_ref)


def coefficient(nr, nq, q, rows, packs, held):
    for k in range(nq):
        held[k ^ q] = packs[k][BW : BW + 8, :]
    trace = rows[0, BW + 1 : BW + 2, :]
    norm = rows[0, BW + 2 : BW + 3, :]
    inner = rows[0, BW + 3 : BW + 4, :]
    for r in range(1, nr):
        trace = trace + rows[r, BW + 1 : BW + 2, :]
        norm = norm + rows[r, BW + 2 : BW + 3, :]
        inner = inner + rows[r, BW + 3 : BW + 4, :]
    for k in range(nq):
        norm = norm + held[k, 1:2, :]
        inner = inner + held[k, 2:3, :]
    c = (norm - inner) / (trace - norm)
    return c, 1.0 / (1.0 - c)


def cross_kernel(nr, nq, ids, lists, rows, *refs):
    packs, refs = refs[:nq], refs[nq:]
    d_old, u_old, su_old, v_old, coef, d_ref, u_ref, su_ref, v_ref, pack_ref, held = refs
    c, inv = coefficient(nr, nq, ids[1], rows, packs, held)
    coef[0:1, :] = c
    coef[1:2, :] = inv
    coef[2:8, :] = jnp.zeros((6, BW), f32)
    for r in range(nr):
        s0, k0 = unpack_pair(rows[r, 0:BW, :], rows[r, BW : BW + 1, :])
        d = d_old[r]
        d_ref[r] = ((1.0 - 2.0 * c) * d + (1.0 + c) * s0 - k0) * inv
    for e in range(nr):
        lo, hi = edge_ends(lists, nq, e)
        s0, _ = unpack_pair(rows[hi, 0:BW, :], rows[hi, BW : BW + 1, :])
        u, su = u_old[e], su_old[e]
        k = dotf(u, s0) + v_old[e]
        u_ref[e] = ((1.0 - 2.0 * c) * u + (1.0 + c) * su - k) * inv
    cross_tail(nr, nq, ids, lists, d_ref, u_ref, su_ref, v_ref, pack_ref)


def last_kernel(nr, nq, ids, lists, coef, *refs):
    packs, refs = refs[:nq], refs[nq:]
    own_pack, x_old, y_old, m_old, link, d_ref, u_ref, su_ref, v_ref = refs[:9]
    x_out, y_out, sums, held, m_ref, mh, ml, col, sq, sqh, sql = refs[9:]
    r, q = ids[0], ids[1]
    assemble(nq, q, coef, packs, x_old, y_old, m_old, held, m_ref, mh, ml)
    g, e = unpack_pair(own_pack[0:BW, :], own_pack[BW : BW + 1, :])
    sq[...] = dot3(mh[...], ml[...], mh[:, at(q)], ml[:, at(q)])
    for a in range(nq):
        sq[cut(a), :] = sq[cut(a), :] * link[a : a + 1, at(q)]
    sq[at(q), :] = sq[at(q), :] + g
    hi, lo = split(sq[...])
    sqh[...] = hi
    sql[...] = lo
    d = m_ref[q]
    s0 = sq[at(q), :]
    col[...] = dot3(mh[...], ml[...], hi, lo)
    k0 = col[at(q), :] + dotf(g, d) + e
    i, j = row_col()
    sums[0:1, :] = total(jnp.where(i == j, d - s0, 0.0))
    sums[1:2, :] = total(jnp.where(i == j, s0 - k0, 0.0))
    sums[2:8, :] = jnp.zeros((6, BW), f32)
    x_out[0] = (d + s0) - k0
    y_out[0] = s0 - 2.0 * d
    for t in range(1, NEAR):
        if t < 6:
            a = lax.rem(q + jnp.int32(offsets(0, nq)[t] + nq), jnp.int32(nq))
        else:
            step = jnp.where(lax.rem(q, jnp.int32(2)) == 0, 3, nq - 3)
            a = lax.rem(q + step, jnp.int32(nq))
        m = mh[at(a), at(q)].astype(f32) + ml[at(a), at(q)].astype(f32)
        s = sq[at(a), :]
        x_out[t] = (m + s) - col[at(a), :]
        y_out[t] = s - 2.0 * m
    sh, sl = split(s0)
    for t in (7, 8):
        far = lax.div(lists[r, t], jnp.int32(nq))
        edge = r if t == 8 else far
        u, su = u_ref[edge], su_ref[edge]
        k = dot3(*split(u), sh, sl) + v_ref[edge]
        x_out[t] = (u + su) - k
        y_out[t] = su - 2.0 * u


def finish_kernel(slots, lists, ids, parts, x_ref, y_ref, out_ref):
    sums = jnp.sum(parts[...], axis=0, keepdims=True)
    half = BW // 2
    low = jnp.broadcast_to(sums[:, 0:1], (1, BW))
    high = jnp.broadcast_to(sums[:, half : half + 1], (1, BW))
    c = high / low
    inv = 1.0 / (1.0 - c)
    r = ids[0]
    own = lists[r, 0]
    for t in range(slots):
        a = lists[r, t]
        keep = jnp.logical_and(a >= 0, a <= own)
        out_ref[0, t] = jnp.where(keep, (x_ref[t] + c * y_ref[t]) * inv, 0.0)


def room(args, outs, scratch):
    sizes = [math.prod(a.shape) * a.dtype.itemsize for a in args]
    sizes += [math.prod(s) * jnp.dtype(d).itemsize for s, d in outs]
    sizes += [math.prod(s.shape) * jnp.dtype(s.dtype).itemsize for s in scratch]
    return min(sum(sizes) + SPARE, MOST)


def call(kernel, outs, args, scalars, scratch=(), flops=0):
    specs = [
        pl.BlockSpec(memory_space=pltpu.SMEM if i < scalars else pltpu.VMEM)
        for i in range(len(args))
    ]
    return pl.pallas_call(
        kernel,
        out_shape=[jax.ShapeDtypeStruct(s, d) for s, d in outs],
        in_specs=specs,
        out_specs=[pl.BlockSpec(memory_space=pltpu.VMEM) for _ in outs],
        scratch_shapes=list(scratch),
        compiler_params=pltpu.CompilerParams(vmem_limit_bytes=room(args, outs, scratch)),
        cost_estimate=pl.CostEstimate(flops=flops, bytes_accessed=0, transcendentals=0),
    )(*args)


def spread(x, nq):
    return [x] + [
        lax.ppermute(x, "col", [(i, i ^ k) for i in range(nq)]) for k in range(1, nq)
    ]


def body(upper_blocks, members):
    nr, nq = lax.axis_size("row"), lax.axis_size("col")
    blocks = upper_blocks[0]
    slots = blocks.shape[0]
    order = nq * BW
    npair = len(pattern(nq))
    ids = jnp.stack([lax.axis_index("row"), lax.axis_index("col")]).astype(jnp.int32)

    flat = blocks.reshape(slots * BW, BW)
    names = jnp.pad(members.astype(f32), ((0, 7), (0, BW - slots)))
    row_part = jnp.concatenate([flat[:BW], flat[NEAR * BW :], names])
    near_part = jnp.concatenate([flat[: NEAR * BW], names])
    row = lax.all_gather(row_part, "row", axis=0)
    near = lax.all_gather(near_part, "col", axis=0)
    lists = row[:, 3 * BW, :slots].astype(jnp.int32)

    listed = (npair, BW, BW)
    dense = (order, order)
    edges = (nr, BW, BW)
    pack = (PACK, BW)
    cross_outs = [(edges, f32)] * 4 + [(pack, f32)]
    square_outs = [(listed, f32), (dense, bf16), (dense, bf16), (pack, f32)]

    d, u, su, v, own = call(
        functools.partial(cross_first_kernel, nr, nq), cross_outs, (ids, lists, row), 2
    )
    packs = spread(own, nq)
    m, mh, ml, link, s, sh, sl, tell = call(
        functools.partial(first_kernel, nq),
        [(listed, f32), (dense, bf16), (dense, bf16), ((nq, order), f32)] + square_outs,
        (ids, near, own),
        1,
    )
    for step in range(PURIFY - 1):
        rows = lax.all_gather(tell, "row", axis=0)
        x, y = call(
            functools.partial(cube_kernel, nq),
            [(listed, f32)] * 2,
            (m, mh, ml, s, sh, sl, link),
            0,
        )
        coef, d, u, su, v, own = call(
            functools.partial(cross_kernel, nr, nq),
            [((8, BW), f32)] + cross_outs,
            (ids, lists, rows, *packs, d, u, su, v),
            2,
            [pltpu.VMEM((nq, 8, BW), f32)],
        )
        old = packs
        if step < PURIFY - 2:
            packs = spread(own, nq)
            m, mh, ml, s, sh, sl, tell = call(
                functools.partial(next_kernel, nq),
                [(listed, f32), (dense, bf16), (dense, bf16)] + square_outs,
                (ids, coef, *old, own, x, y, m, link),
                1,
                [pltpu.VMEM((nq, PACK, BW), f32)],
            )
    strip = (order, BW)
    xo, yo, sums = call(
        functools.partial(last_kernel, nr, nq),
        [((slots, BW, BW), f32)] * 2 + [((8, BW), f32)],
        (ids, lists, coef, *old, own, x, y, m, link, d, u, su, v),
        2,
        [
            pltpu.VMEM((nq, PACK, BW), f32),
            pltpu.VMEM(listed, f32),
            pltpu.VMEM(dense, bf16),
            pltpu.VMEM(dense, bf16),
            pltpu.VMEM(strip, f32),
            pltpu.VMEM(strip, f32),
            pltpu.VMEM(strip, bf16),
            pltpu.VMEM(strip, bf16),
        ],
    )
    lane = jnp.arange(BW) < BW // 2
    mine = jnp.where(lane, sums[0], sums[1])
    parts = lax.all_to_all(
        jnp.broadcast_to(mine[None], (nr * nq, BW)), ("row", "col"), 0, 0, tiled=True
    )
    (out,) = call(
        functools.partial(finish_kernel, slots),
        [((1, slots, BW, BW), f32)],
        (lists, ids, parts, xo, yo),
        2,
    )
    return out


def solution(mesh):
    return jax.shard_map(
        body,
        mesh=mesh,
        in_specs=(P(("row", "col"), None, None, None), P(("row", "col"), None)),
        out_specs=P(("row", "col"), None, None, None),
        check_vma=False,
    )
```

```python
import functools
import math

import jax
import jax.numpy as jnp
from jax import lax
from jax.experimental import pallas as pl
from jax.experimental.pallas import tpu as pltpu
from jax.sharding import PartitionSpec as P

PURIFY = 3
BW = 128
TILE = 256
NEAR = 7
PACK = BW + 8
SPARE = 8 * 1024 * 1024
MOST = 60 * 1024 * 1024

f32 = jnp.float32
bf16 = jnp.bfloat16


def offsets(q, nq):
    return [0, -1, 1, -2, 2, nq // 2, 3 if q % 2 == 0 else -3]


@functools.lru_cache
def pattern(nq):
    pairs = [(q, q) for q in range(nq)]
    for b in range(nq):
        for d in offsets(b, nq)[1:]:
            a = (b + d) % nq
            if a < b:
                pairs.append((a, b))
    return tuple(pairs)


@functools.lru_cache
def pair_index(nq):
    return {pair: i for i, pair in enumerate(pattern(nq))}


def slot_of(a, b, nq):
    return [(b + d) % nq for d in offsets(b, nq)].index(a)


@functools.lru_cache
def tiles(nq):
    index = pair_index(nq)
    n = nq * BW // TILE
    per = TILE // BW

    def live(i, j):
        lo, hi = min(i, j), max(i, j)
        return any(
            (a, b) in index or (b, a) in index
            for a in range(lo * per, (lo + 1) * per)
            for b in range(hi * per, (hi + 1) * per)
        )

    out = []
    for i in range(n):
        for j in range(i, n):
            if live(i, j):
                inner = [k for k in range(n) if live(i, k) and live(k, j)]
                out.append((i, j, inner))
    return out


SHARE = 4


@functools.lru_cache
def shares(nq):
    stored = []
    for b in range(nq):
        slots = [t for t, d in enumerate(offsets(b, nq)) if (b + d) % nq <= b]
        stored.append(slots)
    keep = [slots[:SHARE] for slots in stored]
    give = [slots[SHARE:] for slots in stored]
    donors = sorted((b for b in range(nq) if give[b]), key=lambda b: (-len(give[b]), -b))
    takers = sorted((b for b in range(nq) if len(keep[b]) < SHARE), key=lambda b: len(keep[b]))
    moves = list(zip(donors, takers))
    pair = lambda b, t: ((b + offsets(b, nq)[t]) % nq, b)
    held = [[pair(b, t) for t in keep[b]] for b in range(nq)]
    for donor, taker in moves:
        held[taker] += [pair(donor, t) for t in give[donor]]
    assert len(donors) == len(takers) and all(len(h) == SHARE for h in held)
    return keep, give, moves, held


def split(x):
    hi = x.astype(bf16)
    return hi, (x - hi.astype(f32)).astype(bf16)


def mm(a, b):
    return jnp.dot(a, b, preferred_element_type=f32)


def dot3(ah, al, bh, bl):
    return mm(ah, bh) + (mm(ah, bl) + mm(al, bh))


def dotf(a, b):
    return dot3(*split(a), *split(b))


def row_col():
    return (
        lax.broadcasted_iota(jnp.int32, (BW, BW), 0),
        lax.broadcasted_iota(jnp.int32, (BW, BW), 1),
    )


def total(x):
    s = jnp.sum(jnp.sum(x, axis=0, keepdims=True), axis=1, keepdims=True)
    return jnp.broadcast_to(s, (1, BW))


def pack_pair(ref, first, second):
    i, j = row_col()
    ref[0:BW, :] = jnp.where(i <= j, first, second)
    ref[BW : BW + 1, :] = jnp.sum(jnp.where(i == j, second, 0.0), axis=0, keepdims=True)


def unpack_pair(block, diagonal):
    i, j = row_col()
    flipped = block.T
    first = jnp.where(i <= j, block, flipped)
    second = jnp.where(i > j, block, jnp.where(i == j, diagonal, flipped))
    return first, second


def at(q):
    return pl.ds(pl.multiple_of(q * BW, BW), BW)


def cut(q):
    return slice(q * BW, (q + 1) * BW)


def settle(nq, q, parts, held, rows=slice(None)):
    if len(parts) == 1:
        for k in range(nq):
            held[k] = parts[0][k, rows, :]
        return
    half = nq // 2
    for k in range(half):
        for side in range(2):
            source = lax.rem((q ^ side) + (nq - 2 * k), jnp.int32(nq))
            held[source] = parts[half * side + k][rows, :]


def put_dense(hi_ref, lo_ref, a, b, block):
    hi, lo = split(block)
    hi_ref[cut(a), cut(b)] = hi
    lo_ref[cut(a), cut(b)] = lo
    if a != b:
        hi, lo = split(block.T)
        hi_ref[cut(b), cut(a)] = hi
        lo_ref[cut(b), cut(a)] = lo


def clear_unlinked(hi_ref, lo_ref, nq):
    index = pair_index(nq)
    zero = jnp.zeros((BW, BW), bf16)
    for a in range(nq):
        for b in range(nq):
            if (min(a, b), max(a, b)) not in index:
                hi_ref[cut(a), cut(b)] = zero
                lo_ref[cut(a), cut(b)] = zero


def tile_products(ah, al, bh, bl, nq):
    index = pair_index(nq)
    per = TILE // BW
    n = nq * BW // TILE
    for i, j, inner in tiles(nq):
        rows, cols = slice(i * TILE, (i + 1) * TILE), slice(j * TILE, (j + 1) * TILE)
        if len(inner) == n:
            acc = dot3(ah[rows, :], al[rows, :], bh[:, cols], bl[:, cols])
        else:
            acc = None
            for k in inner:
                mid = slice(k * TILE, (k + 1) * TILE)
                part = dot3(ah[rows, mid], al[rows, mid], bh[mid, cols], bl[mid, cols])
                acc = part if acc is None else acc + part
        for x in range(per):
            for y in range(per):
                a, b = i * per + x, j * per + y
                if (a, b) in index:
                    yield (a, b), acc[cut(x), cut(y)]


def square_part(nq, q, own_pack, m_ref, mh, ml, link, s_ref, sh, sl, out_ref):
    index = pair_index(nq)
    clear_unlinked(sh, sl, nq)
    trace = jnp.zeros((BW, BW), f32)
    norm = jnp.zeros((BW, BW), f32)
    inner = jnp.zeros((BW, BW), f32)
    i, j = row_col()
    for (a, b), block in tile_products(mh, ml, mh, ml, nq):
        if a != b:
            block = block * link[a : a + 1, cut(b)]
        at_list = index[(a, b)]
        s_ref[at_list] = block
        put_dense(sh, sl, a, b, block)
        own = m_ref[at_list]
        if a == b:
            trace = trace + own
            norm = norm + own * own
            inner = inner + own * block
        else:
            norm = norm + 2.0 * (own * own)
            inner = inner + 2.0 * (own * block)
    g, e = unpack_pair(own_pack[0:BW, :], own_pack[BW : BW + 1, :])
    d = m_ref[q]
    dg = dotf(d, g)
    s0 = s_ref[q] + g
    k0 = dot3(mh[at(q), :], ml[at(q), :], sh[:, at(q)], sl[:, at(q)]) + (dg + dg.T) + e
    pack_pair(out_ref, s0, k0)
    out_ref[BW + 1 : BW + 2, :] = total(jnp.where(i == j, trace, 0.0))
    out_ref[BW + 2 : BW + 3, :] = total(norm)
    out_ref[BW + 3 : BW + 4, :] = total(inner)
    out_ref[BW + 4 : BW + 8, :] = jnp.zeros((4, BW), f32)


def choose(q, values):
    out = jnp.int32(values[0])
    for i, v in enumerate(values[1:], 1):
        if v != values[0]:
            out = jnp.where(q == i, jnp.int32(v), out)
    return out


def prepare_kernel(nq, width, ids, names, blocks, near, extra, row):
    q = ids[1]
    keep, give, _, _ = shares(nq)
    lane = lax.broadcasted_iota(jnp.int32, (1, BW), 1)
    listed = jnp.zeros((1, BW), f32)
    for t in range(names.shape[1]):
        listed = jnp.where(lane == t, names[0, t].astype(f32), listed)
    listed = jnp.broadcast_to(listed, (8, BW))
    for i in range(SHARE):
        near[cut(i), :] = blocks[choose(q, [k[min(i, len(k) - 1)] for k in keep])]
    near[SHARE * BW :, :] = listed
    for i in range(width):
        extra[cut(i), :] = blocks[choose(q, [(g + [0] * width)[i] for g in give])]
    for i, t in enumerate((0, NEAR, NEAR + 1)):
        row[cut(i), :] = blocks[t]
    row[3 * BW :, :] = listed


def share_kernel(nq, width, ids, near, moved, own_pack, out):
    q = ids[1]
    count = choose(q, [len(k) for k in shares(nq)[0]])
    out[0 : SHARE * BW + 8, :] = near[...]
    out[SHARE * BW + 8 :, :] = own_pack[...]
    for i in range(1, SHARE):

        @pl.when(i >= count)
        def _():
            out[cut(i), :] = moved[pl.ds(pl.multiple_of((i - count) * BW, BW), BW), :]


def first_kernel(nq, ids, *refs):
    parts, refs = refs[:nq], refs[nq:]
    own_pack, m_ref, mh, ml, link, s_ref, sh, sl, out_ref, packs, near = refs
    q = ids[1]
    settle(nq, q, parts, near)
    for b in range(nq):
        packs[b] = near[b, SHARE * BW + 8 :, :]
    clear_unlinked(mh, ml, nq)
    link[...] = jnp.zeros_like(link)
    index = pair_index(nq)
    for b, pairs in enumerate(shares(nq)[3]):
        for i, pair in enumerate(pairs):
            block = near[b, cut(i), :]
            m_ref[index[pair]] = block
            put_dense(mh, ml, *pair, block)
    for a in range(nq):
        listed = near[a, SHARE * BW : SHARE * BW + 1, :]
        present = jnp.where(listed >= 0.0, 1.0, 0.0)
        for t, d in enumerate(offsets(a, nq)):
            b = (a + d) % nq
            link[a : a + 1, cut(b)] = jnp.broadcast_to(present[:, t : t + 1], (1, BW))
    square_part(nq, q, own_pack, m_ref, mh, ml, link, s_ref, sh, sl, out_ref)


def assemble(nq, q, coef, packs, x_ref, y_ref, m_old, held, m_ref, mh, ml):
    index = pair_index(nq)
    c = coef[0:1, :]
    inv = coef[1:2, :]
    settle(nq, q, packs, held)
    clear_unlinked(mh, ml, nq)
    for b in range(nq):
        g, e = unpack_pair(held[b, 0:BW, :], held[b, BW : BW + 1, :])
        gh, gl = split(g)
        for (a, b2), place in index.items():
            if b2 != b:
                continue
            fix = dot3(*split(m_old[place]), gh, gl)
            block = x_ref[place] + c * y_ref[place]
            if a == b:
                block = block + (1.0 + c) * g - (fix + fix.T + e)
            else:
                block = block - fix
            block = block * inv
            m_ref[place] = block
            put_dense(mh, ml, a, b, block)


def next_kernel(nq, count, ids, coef, *refs):
    packs, own_pack, refs = refs[:count], refs[count], refs[count + 1 :]
    x_ref, y_ref, m_old, link, m_ref, mh, ml, s_ref, sh, sl, out_ref, held = refs
    q = ids[1]
    assemble(nq, q, coef, packs, x_ref, y_ref, m_old, held, m_ref, mh, ml)
    square_part(nq, q, own_pack, m_ref, mh, ml, link, s_ref, sh, sl, out_ref)


def cube_kernel(nq, m_ref, mh, ml, s_ref, sh, sl, link, x_ref, y_ref):
    index = pair_index(nq)
    for (a, b), block in tile_products(mh, ml, sh, sl, nq):
        if a != b:
            block = block * link[a : a + 1, cut(b)]
        place = index[(a, b)]
        m, s = m_ref[place], s_ref[place]
        x_ref[place] = (m + s) - block
        y_ref[place] = s - 2.0 * m


def far_row(lists, r, nq, e, slot):
    return lax.div(lists[e ^ r, slot], jnp.int32(nq))


def edge_ends(lists, r, nq, e):
    far = far_row(lists, r, nq, e, 8)
    return jnp.minimum(far, e), jnp.maximum(far, e)


def cross_tail(nr, nq, ids, lists, d_ref, u_ref, su_ref, v_ref, pack_ref):
    r = ids[0]
    norm = jnp.zeros((BW, BW), f32)
    inner = jnp.zeros((BW, BW), f32)
    for e in range(nr):
        lo, hi = edge_ends(lists, r, nq, e)
        u = u_ref[e]
        uh, ul = split(u)
        dlo = split(d_ref[lo])
        su = dot3(uh, ul, *split(d_ref[hi])) + dot3(*dlo, uh, ul)
        su_ref[e] = su
        v_ref[e] = dot3(*dlo, *split(su))
        norm = norm + u * u
        inner = inner + u * su
    g_sum = jnp.zeros((BW, BW), f32)
    e_sum = jnp.zeros((BW, BW), f32)
    for slot in (7, 8):
        far = far_row(lists, r, nq, r, slot)
        u = u_ref[r if slot == 8 else far]
        flipped = u.T
        mine = r > far
        cu = split(jnp.where(mine, u, flipped))
        cut_ = split(jnp.where(mine, flipped, u))
        g_sum = g_sum + dot3(*cut_, *cu)
        t = dot3(*split(d_ref[far]), *cu)
        e_sum = e_sum + dot3(*cut_, *split(t))
    pack_pair(pack_ref, g_sum, e_sum)
    pack_ref[BW + 1 : BW + 2, :] = 2.0 * total(norm)
    pack_ref[BW + 2 : BW + 3, :] = 3.0 * total(inner)
    pack_ref[BW + 3 : BW + 8, :] = jnp.zeros((5, BW), f32)


def cross_first_kernel(nr, nq, ids, lists, *refs):
    parts, refs = refs[:nr], refs[nr:]
    d_ref, u_ref, su_ref, v_ref, pack_ref, row = refs
    r = ids[0]
    for k in range(nr):
        row[k ^ r] = parts[k][...]
    for e in range(nr):
        d_ref[e] = row[e, cut(0), :]
    for e in range(nr):
        far = far_row(lists, r, nq, e, 8)
        here = row[e, cut(2), :]
        there = row[far, cut(1), :]
        u_ref[e] = jnp.where(far < e, here, there)
    cross_tail(nr, nq, ids, lists, d_ref, u_ref, su_ref, v_ref, pack_ref)


def coefficient(nr, nq, q, rows, packs, held):
    settle(nq, q, packs, held, slice(BW, BW + 8))
    trace = rows[0, BW + 1 : BW + 2, :]
    norm = rows[0, BW + 2 : BW + 3, :]
    inner = rows[0, BW + 3 : BW + 4, :]
    for r in range(1, nr):
        trace = trace + rows[r, BW + 1 : BW + 2, :]
        norm = norm + rows[r, BW + 2 : BW + 3, :]
        inner = inner + rows[r, BW + 3 : BW + 4, :]
    for k in range(nq):
        norm = norm + held[k, 1:2, :]
        inner = inner + held[k, 2:3, :]
    c = (norm - inner) / (trace - norm)
    return c, 1.0 / (1.0 - c)


def cross_kernel(nr, nq, count, ids, lists, *refs):
    parts, packs, refs = refs[:nr], refs[nr : nr + count], refs[nr + count :]
    d_old, u_old, su_old, v_old, coef, d_ref, u_ref, su_ref, v_ref, pack_ref, held, rows = refs
    r = ids[0]
    for k in range(nr):
        rows[k ^ r] = parts[k][...]
    c, inv = coefficient(nr, nq, ids[1], rows, packs, held)
    coef[0:1, :] = c
    coef[1:2, :] = inv
    coef[2:8, :] = jnp.zeros((6, BW), f32)
    for p in range(nr):
        s0, k0 = unpack_pair(rows[p, 0:BW, :], rows[p, BW : BW + 1, :])
        d = d_old[p]
        d_ref[p] = ((1.0 - 2.0 * c) * d + (1.0 + c) * s0 - k0) * inv
    for e in range(nr):
        lo, hi = edge_ends(lists, r, nq, e)
        s0, _ = unpack_pair(rows[hi, 0:BW, :], rows[hi, BW : BW + 1, :])
        u, su = u_old[e], su_old[e]
        k = dotf(u, s0) + v_old[e]
        u_ref[e] = ((1.0 - 2.0 * c) * u + (1.0 + c) * su - k) * inv
    cross_tail(nr, nq, ids, lists, d_ref, u_ref, su_ref, v_ref, pack_ref)


def last_kernel(nr, nq, count, ids, lists, coef, *refs):
    packs, refs = refs[:count], refs[count:]
    own_pack, x_old, y_old, m_old, link, d_ref, u_ref, su_ref, v_ref = refs[:9]
    x_out, y_out, sums, held, m_ref, mh, ml, col, sq, sqh, sql = refs[9:]
    r, q = ids[0], ids[1]
    assemble(nq, q, coef, packs, x_old, y_old, m_old, held, m_ref, mh, ml)
    g, e = unpack_pair(own_pack[0:BW, :], own_pack[BW : BW + 1, :])
    sq[...] = dot3(mh[...], ml[...], mh[:, at(q)], ml[:, at(q)])
    for a in range(nq):
        sq[cut(a), :] = sq[cut(a), :] * link[a : a + 1, at(q)]
    sq[at(q), :] = sq[at(q), :] + g
    hi, lo = split(sq[...])
    sqh[...] = hi
    sql[...] = lo
    d = m_ref[q]
    s0 = sq[at(q), :]
    col[...] = dot3(mh[...], ml[...], hi, lo)
    k0 = col[at(q), :] + dotf(g, d) + e
    i, j = row_col()
    sums[0:1, :] = total(jnp.where(i == j, d - s0, 0.0))
    sums[1:2, :] = total(jnp.where(i == j, s0 - k0, 0.0))
    sums[2:8, :] = jnp.zeros((6, BW), f32)
    x_out[0] = (d + s0) - k0
    y_out[0] = s0 - 2.0 * d
    for t in range(1, NEAR):
        if t < 6:
            a = lax.rem(q + jnp.int32(offsets(0, nq)[t] + nq), jnp.int32(nq))
        else:
            step = jnp.where(lax.rem(q, jnp.int32(2)) == 0, 3, nq - 3)
            a = lax.rem(q + step, jnp.int32(nq))
        m = mh[at(a), at(q)].astype(f32) + ml[at(a), at(q)].astype(f32)
        s = sq[at(a), :]
        x_out[t] = (m + s) - col[at(a), :]
        y_out[t] = s - 2.0 * m
    sh, sl = split(s0)
    for t in (7, 8):
        far = far_row(lists, r, nq, r, t)
        edge = r if t == 8 else far
        u, su = u_ref[edge], su_ref[edge]
        k = dot3(*split(u), sh, sl) + v_ref[edge]
        x_out[t] = (u + su) - k
        y_out[t] = su - 2.0 * u


def finish_kernel(slots, lists, ids, parts, x_ref, y_ref, out_ref):
    sums = jnp.sum(parts[...], axis=0, keepdims=True)
    half = BW // 2
    low = jnp.broadcast_to(sums[:, 0:1], (1, BW))
    high = jnp.broadcast_to(sums[:, half : half + 1], (1, BW))
    c = high / low
    inv = 1.0 / (1.0 - c)
    own = lists[0, 0]
    for t in range(slots):
        a = lists[0, t]
        keep = jnp.logical_and(a >= 0, a <= own)
        out_ref[0, t] = jnp.where(keep, (x_ref[t] + c * y_ref[t]) * inv, 0.0)


def room(args, outs, scratch):
    sizes = [math.prod(a.shape) * a.dtype.itemsize for a in args]
    sizes += [math.prod(s) * jnp.dtype(d).itemsize for s, d in outs]
    sizes += [math.prod(s.shape) * jnp.dtype(s.dtype).itemsize for s in scratch]
    return min(sum(sizes) + SPARE, MOST)


def call(kernel, outs, args, scalars, scratch=(), flops=0):
    specs = [
        pl.BlockSpec(memory_space=pltpu.SMEM if i < scalars else pltpu.VMEM)
        for i in range(len(args))
    ]
    return pl.pallas_call(
        kernel,
        out_shape=[jax.ShapeDtypeStruct(s, d) for s, d in outs],
        in_specs=specs,
        out_specs=[pl.BlockSpec(memory_space=pltpu.VMEM) for _ in outs],
        scratch_shapes=list(scratch),
        compiler_params=pltpu.CompilerParams(vmem_limit_bytes=room(args, outs, scratch)),
        cost_estimate=pl.CostEstimate(flops=flops, bytes_accessed=0, transcendentals=0),
    )(*args)


def spread(x, axis, size):
    return [x] + [
        lax.ppermute(x, axis, [(i, i ^ k) for i in range(size)]) for k in range(1, size)
    ]


def gather_near(near, extra, own_pack, ids, width, nq):
    moved = lax.ppermute(extra, "col", shares(nq)[2])
    (own,) = call(
        functools.partial(share_kernel, nq, width),
        [((near.shape[0] + PACK, BW), f32)],
        (ids, near, moved, own_pack),
        1,
    )
    return gather(own, nq)


def gather(x, nq):
    here = [x] + [
        lax.ppermute(x, "col", [(i, (i + 2 * k) % nq) for i in range(nq)])
        for k in range(1, nq // 2)
    ]
    there = [lax.ppermute(y, "col", [(i, i ^ 1) for i in range(nq)]) for y in here]
    return here + there


def body(upper_blocks, members):
    nr, nq = lax.axis_size("row"), lax.axis_size("col")
    blocks = upper_blocks[0]
    slots = blocks.shape[0]
    order = nq * BW
    npair = len(pattern(nq))
    ids = jnp.stack([lax.axis_index("row"), lax.axis_index("col")]).astype(jnp.int32)

    width = max(len(g) for g in shares(nq)[1])
    share = (SHARE * BW + 8, BW)
    near, extra, row_part = call(
        functools.partial(prepare_kernel, nq, width),
        [(share, f32), ((width * BW, BW), f32), ((3 * BW + 8, BW), f32)],
        (ids, members, blocks),
        2,
    )
    row = spread(row_part, "row", nr)
    lists = jnp.concatenate([x[3 * BW : 3 * BW + 1, :slots] for x in row]).astype(jnp.int32)

    square_flops = 6 * order**3
    listed = (npair, BW, BW)
    dense = (order, order)
    edges = (nr, BW, BW)
    pack = (PACK, BW)
    cross_outs = [(edges, f32)] * 4 + [(pack, f32)]
    square_outs = [(listed, f32), (dense, bf16), (dense, bf16), (pack, f32)]

    d, u, su, v, own = call(
        functools.partial(cross_first_kernel, nr, nq), cross_outs, (ids, lists, *row), 2,
        [pltpu.VMEM((nr, 3 * BW + 8, BW), f32)],
    )
    nears = gather_near(near, extra, own, ids, width, nq)
    m, mh, ml, link, s, sh, sl, tell, packs = call(
        functools.partial(first_kernel, nq),
        [(listed, f32), (dense, bf16), (dense, bf16), ((nq, order), f32)]
        + square_outs
        + [((nq,) + pack, f32)],
        (ids, *nears, own),
        1,
        [pltpu.VMEM((nq,) + nears[0].shape, f32)],
        flops=square_flops,
    )
    packs = [packs]
    for step in range(PURIFY - 1):
        rows = spread(tell, "row", nr)
        x, y = call(
            functools.partial(cube_kernel, nq),
            [(listed, f32)] * 2,
            (m, mh, ml, s, sh, sl, link),
            0,
            flops=square_flops,
        )
        coef, d, u, su, v, own = call(
            functools.partial(cross_kernel, nr, nq, len(packs)),
            [((8, BW), f32)] + cross_outs,
            (ids, lists, *rows, *packs, d, u, su, v),
            2,
            [pltpu.VMEM((nq, 8, BW), f32), pltpu.VMEM((nr, PACK, BW), f32)],
            flops=square_flops // 4,
        )
        old = packs
        if step < PURIFY - 2:
            packs = gather(own, nq)
            m, mh, ml, s, sh, sl, tell = call(
                functools.partial(next_kernel, nq, len(old)),
                [(listed, f32), (dense, bf16), (dense, bf16)] + square_outs,
                (ids, coef, *old, own, x, y, m, link),
                1,
                [pltpu.VMEM((nq, PACK, BW), f32)],
                flops=square_flops,
            )
    strip = (order, BW)
    xo, yo, sums = call(
        functools.partial(last_kernel, nr, nq, len(old)),
        [((slots, BW, BW), f32)] * 2 + [((8, BW), f32)],
        (ids, lists, coef, *old, own, x, y, m, link, d, u, su, v),
        2,
        [
            pltpu.VMEM((nq, PACK, BW), f32),
            pltpu.VMEM(listed, f32),
            pltpu.VMEM(dense, bf16),
            pltpu.VMEM(dense, bf16),
            pltpu.VMEM(strip, f32),
            pltpu.VMEM(strip, f32),
            pltpu.VMEM(strip, bf16),
            pltpu.VMEM(strip, bf16),
        ],
    )
    lane = jnp.arange(BW) < BW // 2
    mine = jnp.where(lane, sums[0], sums[1])
    parts = lax.all_to_all(
        jnp.broadcast_to(mine[None], (nr * nq, BW)), ("row", "col"), 0, 0, tiled=True
    )
    (out,) = call(
        functools.partial(finish_kernel, slots),
        [((1, slots, BW, BW), f32)],
        (lists, ids, parts, xo, yo),
        2,
    )
    return out


def solution(mesh):
    return jax.shard_map(
        body,
        mesh=mesh,
        in_specs=(P(("row", "col"), None, None, None), P(("row", "col"), None)),
        out_specs=P(("row", "col"), None, None, None),
        check_vma=False,
    )
```

```python
import functools
import math

import jax
import jax.numpy as jnp
from jax import lax
from jax.experimental import pallas as pl
from jax.experimental.pallas import tpu as pltpu
from jax.sharding import PartitionSpec as P

PURIFY = 3
BW = 128
TILE = 256
NEAR = 7
PACK = BW + 8
SPARE = 8 * 1024 * 1024
MOST = 60 * 1024 * 1024

f32 = jnp.float32
bf16 = jnp.bfloat16


def offsets(q, nq):
    return [0, -1, 1, -2, 2, nq // 2, 3 if q % 2 == 0 else -3]


@functools.lru_cache
def pattern(nq):
    pairs = [(q, q) for q in range(nq)]
    for b in range(nq):
        for d in offsets(b, nq)[1:]:
            a = (b + d) % nq
            if a < b:
                pairs.append((a, b))
    return tuple(pairs)


@functools.lru_cache
def pair_index(nq):
    return {pair: i for i, pair in enumerate(pattern(nq))}


def slot_of(a, b, nq):
    return [(b + d) % nq for d in offsets(b, nq)].index(a)


@functools.lru_cache
def tiles(nq):
    index = pair_index(nq)
    n = nq * BW // TILE
    per = TILE // BW

    def live(i, j):
        lo, hi = min(i, j), max(i, j)
        return any(
            (a, b) in index or (b, a) in index
            for a in range(lo * per, (lo + 1) * per)
            for b in range(hi * per, (hi + 1) * per)
        )

    out = []
    for i in range(n):
        for j in range(i, n):
            if live(i, j):
                inner = [k for k in range(n) if live(i, k) and live(k, j)]
                out.append((i, j, inner))
    return out


PAIR = 8
FEW, SOME, ALL = 4, 5, 7
FRONT = 5
NAMES = FRONT * BW
TERMS = 16 + PAIR * BW
HALF = NAMES + 16


@functools.lru_cache
def stored(nq):
    out = []
    for b in range(nq):
        out.append([t for t, d in enumerate(offsets(b, nq)) if (b + d) % nq <= b])
    for b in range(nq // 2):
        assert len(out[b]) <= FEW and len(out[b]) + len(out[nq - 1 - b]) == PAIR
    return out


def counts(nq):
    return [len(stored(nq)[nq - 1 - p]) for p in range(nq // 2)]


def pair_blocks(nq, p):
    return [
        ((b + offsets(b, nq)[t]) % nq, b) for b in (nq - 1 - p, p) for t in stored(nq)[b]
    ]


def split(x):
    hi = x.astype(bf16)
    return hi, (x - hi.astype(f32)).astype(bf16)


def mm(a, b):
    return jnp.dot(a, b, preferred_element_type=f32)


def dot3(ah, al, bh, bl):
    if bh.shape[1] != BW:
        return mm(ah, bh) + (mm(ah, bl) + mm(al, bh))
    if bh.shape[0] == BW:
        top = jnp.concatenate([bh, bl], axis=1)
        low = jnp.concatenate([bh, jnp.zeros_like(bl)], axis=1)
        both = mm(jnp.concatenate([ah, al], axis=1), jnp.concatenate([top, low], axis=0))
        return both[:, :BW] + both[:, BW:]
    both = mm(ah, jnp.concatenate([bh, bl], axis=1))
    return both[:, :BW] + (both[:, BW:] + mm(al, bh))


def dotf(a, b):
    return dot3(*split(a), *split(b))


def row_col():
    return (
        lax.broadcasted_iota(jnp.int32, (BW, BW), 0),
        lax.broadcasted_iota(jnp.int32, (BW, BW), 1),
    )


def total(x):
    s = jnp.sum(jnp.sum(x, axis=0, keepdims=True), axis=1, keepdims=True)
    return jnp.broadcast_to(s, (1, BW))


def pack_pair(ref, first, second):
    i, j = row_col()
    ref[0:BW, :] = jnp.where(i <= j, first, second)
    ref[BW : BW + 1, :] = jnp.sum(jnp.where(i == j, second, 0.0), axis=0, keepdims=True)


def unpack_pair(block, diagonal):
    i, j = row_col()
    flipped = block.T
    first = jnp.where(i <= j, block, flipped)
    second = jnp.where(i > j, block, jnp.where(i == j, diagonal, flipped))
    return first, second


def at(q):
    return pl.ds(pl.multiple_of(q * BW, BW), BW)


def cut(q):
    return slice(q * BW, (q + 1) * BW)


def settle(nq, q, parts, held, rows=slice(None)):
    if len(parts) == 1:
        for k in range(nq):
            held[k] = parts[0][k, rows, :]
        return
    half = nq // 2
    for k in range(half):
        for side in range(2):
            source = lax.rem((q ^ side) + (nq - 2 * k), jnp.int32(nq))
            held[source] = parts[half * side + k][rows, :]


def put_dense(hi_ref, lo_ref, a, b, block):
    hi, lo = split(block)
    hi_ref[cut(a), cut(b)] = hi
    lo_ref[cut(a), cut(b)] = lo
    if a != b:
        hi, lo = split(block.T)
        hi_ref[cut(b), cut(a)] = hi
        lo_ref[cut(b), cut(a)] = lo


def clear_unlinked(hi_ref, lo_ref, nq):
    index = pair_index(nq)
    zero = jnp.zeros((BW, BW), bf16)
    for a in range(nq):
        for b in range(nq):
            if (min(a, b), max(a, b)) not in index:
                hi_ref[cut(a), cut(b)] = zero
                lo_ref[cut(a), cut(b)] = zero


def tile_products(ah, al, bh, bl, nq):
    index = pair_index(nq)
    per = TILE // BW
    n = nq * BW // TILE
    for i, j, inner in tiles(nq):
        rows, cols = slice(i * TILE, (i + 1) * TILE), slice(j * TILE, (j + 1) * TILE)
        if len(inner) == n:
            acc = dot3(ah[rows, :], al[rows, :], bh[:, cols], bl[:, cols])
        else:
            acc = None
            for k in inner:
                mid = slice(k * TILE, (k + 1) * TILE)
                part = dot3(ah[rows, mid], al[rows, mid], bh[mid, cols], bl[mid, cols])
                acc = part if acc is None else acc + part
        for x in range(per):
            for y in range(per):
                a, b = i * per + x, j * per + y
                if (a, b) in index:
                    yield (a, b), acc[cut(x), cut(y)]


def square_part(nq, q, own_pack, m_ref, mh, ml, link, s_ref, sh, sl, out_ref):
    index = pair_index(nq)
    clear_unlinked(sh, sl, nq)
    trace = jnp.zeros((BW, BW), f32)
    norm = jnp.zeros((BW, BW), f32)
    inner = jnp.zeros((BW, BW), f32)
    i, j = row_col()
    for (a, b), block in tile_products(mh, ml, mh, ml, nq):
        if a != b:
            block = block * link[a : a + 1, cut(b)]
        at_list = index[(a, b)]
        s_ref[at_list] = block
        put_dense(sh, sl, a, b, block)
        own = m_ref[at_list]
        if a == b:
            trace = trace + own
            norm = norm + own * own
            inner = inner + own * block
        else:
            norm = norm + 2.0 * (own * own)
            inner = inner + 2.0 * (own * block)
    g, e = unpack_pair(own_pack[0:BW, :], own_pack[BW : BW + 1, :])
    d = m_ref[q]
    dg = dotf(d, g)
    s0 = s_ref[q] + g
    k0 = dot3(mh[at(q), :], ml[at(q), :], sh[:, at(q)], sl[:, at(q)]) + (dg + dg.T) + e
    pack_pair(out_ref, s0, k0)
    out_ref[BW + 1 : BW + 2, :] = total(jnp.where(i == j, trace, 0.0))
    out_ref[BW + 2 : BW + 3, :] = total(norm)
    out_ref[BW + 3 : BW + 4, :] = total(inner)
    out_ref[BW + 4 : BW + 8, :] = jnp.zeros((4, BW), f32)


def choose(q, values):
    out = jnp.int32(values[0])
    for i, v in enumerate(values[1:], 1):
        if v != values[0]:
            out = jnp.where(q == i, jnp.int32(v), out)
    return out


def prepare_kernel(nq, ids, names, blocks, most, few, row):
    q = ids[1]
    lane = lax.broadcasted_iota(jnp.int32, (1, BW), 1)
    listed = jnp.zeros((1, BW), f32)
    for t in range(names.shape[1]):
        listed = jnp.where(lane == t, names[0, t].astype(f32), listed)
    listed = jnp.broadcast_to(listed, (8, BW))
    most[0:8, :] = listed
    few[0:8, :] = listed
    for i in range(ALL):
        block = blocks[choose(q, [(slots + [0] * ALL)[i] for slots in stored(nq)])]
        most[place(i), :] = block
        if i < FEW:
            few[place(i), :] = block
    for i, t in enumerate((0, NEAR, NEAR + 1)):
        row[cut(i), :] = blocks[t]
    row[3 * BW :, :] = listed


def place(i):
    return slice(8 + i * BW, 8 + (i + 1) * BW)


def at_place(i):
    return pl.ds(pl.multiple_of(8 + i * BW, 8), BW)


def lay(i):
    start = i * BW + (16 if i >= FRONT else 0)
    return slice(start, start + BW)


def pair_kernel(nq, ids, own, all_in, some_in, few_in, own_pack, pack_in, front, back):
    q = ids[1]
    upper = q >= nq // 2
    count = choose(jnp.where(upper, nq - 1 - q, q), counts(nq))

    def fill(first, second):
        for i in range(PAIR):
            out, rows = (front, lay(i)) if i < FRONT else (back, cut(i - FRONT))
            if i < FEW:
                out[rows, :] = first[place(i), :]
                continue
            if i < (first.shape[0] - 8) // BW:

                @pl.when(i < count)
                def _(out=out, rows=rows, i=i):
                    out[rows, :] = first[place(i), :]

            @pl.when(i >= count)
            def _(out=out, rows=rows, i=i):
                out[rows, :] = second[at_place(i - count), :]

        front[NAMES : NAMES + 8, :] = first[0:8, :]
        front[NAMES + 8 : NAMES + 16, :] = second[0:8, :]

    wide = count > SOME

    @pl.when(upper)
    def _():
        fill(own, few_in)

    @pl.when(jnp.logical_and(jnp.logical_not(upper), wide))
    def _():
        fill(all_in, own)

    @pl.when(jnp.logical_and(jnp.logical_not(upper), jnp.logical_not(wide)))
    def _():
        fill(some_in, own)

    terms = (PAIR - FRONT) * BW
    back[terms : terms + PACK, :] = jnp.where(upper, own_pack[...], pack_in[...])
    back[terms + PACK :, :] = jnp.where(upper, pack_in[...], own_pack[...])


def first_kernel(nq, ids, *refs):
    half = nq // 2
    fronts, backs, refs = refs[:half], refs[half:nq], refs[nq:]
    own_pack, m_ref, mh, ml, link, s_ref, sh, sl, out_ref, packs, near = refs
    q = ids[1]
    own = jnp.minimum(q, nq - 1 - q)
    for m in range(half):
        near[m ^ own, 0:HALF, :] = fronts[m][...]
        near[m ^ own, HALF:, :] = backs[m][...]
    clear_unlinked(mh, ml, nq)
    link[...] = jnp.zeros_like(link)
    index = pair_index(nq)
    for p in range(half):
        packs[nq - 1 - p] = near[p, TERMS : TERMS + PACK, :]
        packs[p] = near[p, TERMS + PACK :, :]
        for i, pair in enumerate(pair_blocks(nq, p)):
            block = near[p, lay(i), :]
            m_ref[index[pair]] = block
            put_dense(mh, ml, *pair, block)
    for a in range(nq):
        row = NAMES if a >= half else NAMES + 8
        listed = near[min(a, nq - 1 - a), row : row + 1, :]
        present = jnp.where(listed >= 0.0, 1.0, 0.0)
        for t, d in enumerate(offsets(a, nq)):
            b = (a + d) % nq
            link[a : a + 1, cut(b)] = jnp.broadcast_to(present[:, t : t + 1], (1, BW))
    square_part(nq, q, own_pack, m_ref, mh, ml, link, s_ref, sh, sl, out_ref)


def assemble(nq, q, c, inv, packs, x_ref, y_ref, m_old, held, m_ref, mh, ml):
    index = pair_index(nq)
    settle(nq, q, packs, held)
    clear_unlinked(mh, ml, nq)
    for b in range(nq):
        g, e = unpack_pair(held[b, 0:BW, :], held[b, BW : BW + 1, :])
        rows = [a for a in range(nq) if (a, b) in index]
        stack = jnp.concatenate([m_old[index[(a, b)]] for a in rows], axis=0)
        fixes = dotf(stack, g)
        for i, a in enumerate(rows):
            fix = fixes[cut(i), :]
            place = index[(a, b)]
            block = x_ref[place] + c * y_ref[place]
            if a == b:
                block = block + (1.0 + c) * g - (fix + fix.T + e)
            else:
                block = block - fix
            block = block * inv
            m_ref[place] = block
            put_dense(mh, ml, a, b, block)


def next_kernel(nq, count, ids, coef, *refs):
    packs, own_pack, refs = refs[:count], refs[count], refs[count + 1 :]
    x_ref, y_ref, m_old, link, m_ref, mh, ml, s_ref, sh, sl, out_ref, held = refs
    q = ids[1]
    assemble(nq, q, coef[0:1, :], coef[1:2, :], packs, x_ref, y_ref, m_old, held, m_ref, mh, ml)
    square_part(nq, q, own_pack, m_ref, mh, ml, link, s_ref, sh, sl, out_ref)


def cube_kernel(nq, m_ref, mh, ml, s_ref, sh, sl, link, x_ref, y_ref):
    index = pair_index(nq)
    for (a, b), block in tile_products(mh, ml, sh, sl, nq):
        if a != b:
            block = block * link[a : a + 1, cut(b)]
        place = index[(a, b)]
        m, s = m_ref[place], s_ref[place]
        x_ref[place] = (m + s) - block
        y_ref[place] = s - 2.0 * m


def far_row(lists, r, nq, e, slot):
    return lax.div(lists[e ^ r, slot], jnp.int32(nq))


def edge_ends(lists, r, nq, e):
    far = far_row(lists, r, nq, e, 8)
    return jnp.minimum(far, e), jnp.maximum(far, e)


def cross_tail(nr, nq, ids, lists, d_ref, u_ref, su_ref, v_ref, pack_ref):
    r = ids[0]
    norm = jnp.zeros((BW, BW), f32)
    inner = jnp.zeros((BW, BW), f32)
    for e in range(nr):
        lo, hi = edge_ends(lists, r, nq, e)
        u = u_ref[e]
        uh, ul = split(u)
        dlo = split(d_ref[lo])
        su = dot3(uh, ul, *split(d_ref[hi])) + dot3(*dlo, uh, ul)
        su_ref[e] = su
        v_ref[e] = dot3(*dlo, *split(su))
        norm = norm + u * u
        inner = inner + u * su
    g_sum = jnp.zeros((BW, BW), f32)
    e_sum = jnp.zeros((BW, BW), f32)
    for slot in (7, 8):
        far = far_row(lists, r, nq, r, slot)
        u = u_ref[r if slot == 8 else far]
        flipped = u.T
        mine = r > far
        cu = split(jnp.where(mine, u, flipped))
        cut_ = split(jnp.where(mine, flipped, u))
        g_sum = g_sum + dot3(*cut_, *cu)
        t = dot3(*split(d_ref[far]), *cu)
        e_sum = e_sum + dot3(*cut_, *split(t))
    pack_pair(pack_ref, g_sum, e_sum)
    pack_ref[BW + 1 : BW + 2, :] = 2.0 * total(norm)
    pack_ref[BW + 2 : BW + 3, :] = 3.0 * total(inner)
    pack_ref[BW + 3 : BW + 8, :] = jnp.zeros((5, BW), f32)


def cross_first_kernel(nr, nq, ids, lists, *refs):
    parts, refs = refs[:nr], refs[nr:]
    d_ref, u_ref, su_ref, v_ref, pack_ref, row = refs
    r = ids[0]
    for k in range(nr):
        row[k ^ r] = parts[k][...]
    for e in range(nr):
        d_ref[e] = row[e, cut(0), :]
    for e in range(nr):
        far = far_row(lists, r, nq, e, 8)
        here = row[e, cut(2), :]
        there = row[far, cut(1), :]
        u_ref[e] = jnp.where(far < e, here, there)
    cross_tail(nr, nq, ids, lists, d_ref, u_ref, su_ref, v_ref, pack_ref)


def coefficient(nr, nq, q, rows, packs, held):
    settle(nq, q, packs, held, slice(BW, BW + 8))
    trace = rows[0, BW + 1 : BW + 2, :]
    norm = rows[0, BW + 2 : BW + 3, :]
    inner = rows[0, BW + 3 : BW + 4, :]
    for r in range(1, nr):
        trace = trace + rows[r, BW + 1 : BW + 2, :]
        norm = norm + rows[r, BW + 2 : BW + 3, :]
        inner = inner + rows[r, BW + 3 : BW + 4, :]
    for k in range(nq):
        norm = norm + held[k, 1:2, :]
        inner = inner + held[k, 2:3, :]
    c = (norm - inner) / (trace - norm)
    return c, 1.0 / (1.0 - c)


def cross_kernel(nr, nq, count, ids, lists, *refs):
    parts, packs, refs = refs[:nr], refs[nr : nr + count], refs[nr + count :]
    d_old, u_old, su_old, v_old, coef, d_ref, u_ref, su_ref, v_ref, pack_ref, held, rows = refs
    r = ids[0]
    for k in range(nr):
        rows[k ^ r] = parts[k][...]
    c, inv = coefficient(nr, nq, ids[1], rows, packs, held)
    coef[0:1, :] = c
    coef[1:2, :] = inv
    coef[2:8, :] = jnp.zeros((6, BW), f32)
    for p in range(nr):
        s0, k0 = unpack_pair(rows[p, 0:BW, :], rows[p, BW : BW + 1, :])
        d = d_old[p]
        d_ref[p] = ((1.0 - 2.0 * c) * d + (1.0 + c) * s0 - k0) * inv
    for e in range(nr):
        lo, hi = edge_ends(lists, r, nq, e)
        s0, _ = unpack_pair(rows[hi, 0:BW, :], rows[hi, BW : BW + 1, :])
        u, su = u_old[e], su_old[e]
        k = dotf(u, s0) + v_old[e]
        u_ref[e] = ((1.0 - 2.0 * c) * u + (1.0 + c) * su - k) * inv
    cross_tail(nr, nq, ids, lists, d_ref, u_ref, su_ref, v_ref, pack_ref)


def last_kernel(nr, nq, count, ids, lists, *refs):
    parts, packs, refs = refs[:nr], refs[nr : nr + count], refs[nr + count :]
    x_old, y_old, m_old, link, d_old, u_old, su_old, v_old = refs[:8]
    x_out, y_out, sums, rows, ends, held, m_ref, mh, ml, col, sq = refs[8:]
    r, q = ids[0], ids[1]
    for k in range(nr):
        rows[k ^ r] = parts[k][...]
    c, inv = coefficient(nr, nq, q, rows, packs, ends)

    def step(p, s, k):
        return ((1.0 - 2.0 * c) * p + (1.0 + c) * s - k) * inv

    def told(p):
        return unpack_pair(rows[p, 0:BW, :], rows[p, BW : BW + 1, :])

    assemble(nq, q, c, inv, packs, x_old, y_old, m_old, held, m_ref, mh, ml)
    d = m_ref[q]
    g = jnp.zeros((BW, BW), f32)
    e = jnp.zeros((BW, BW), f32)
    cross = []
    for slot in (7, 8):
        far = far_row(lists, r, nq, r, slot)
        edge = r if slot == 8 else far
        u, su = u_old[edge], su_old[edge]
        u = step(u, su, dotf(u, told(jnp.maximum(far, r))[0]) + v_old[edge])
        flipped = u.T
        mine = r > far
        cu = jnp.where(mine, u, flipped)
        cut_ = split(jnp.where(mine, flipped, u))
        far_d = split(step(d_old[far], *told(far)))
        t = dot3(*far_d, *split(cu))
        scu = dotf(cu, d) + t
        g = g + dot3(*cut_, *split(cu))
        e = e + dot3(*cut_, *split(t))
        cross.append((slot, cu, scu, dot3(*far_d, *split(scu))))
    sq[...] = dot3(mh[...], ml[...], mh[:, at(q)], ml[:, at(q)])
    for a in range(nq):
        sq[cut(a), :] = sq[cut(a), :] * link[a : a + 1, at(q)]
    sq[at(q), :] = sq[at(q), :] + g
    col[...] = dot3(mh[...], ml[...], *split(sq[...]))
    s0 = sq[at(q), :]
    k0 = col[at(q), :] + dotf(g, d) + e
    i, j = row_col()
    sums[0:1, :] = total(jnp.where(i == j, d - s0, 0.0))
    sums[1:2, :] = total(jnp.where(i == j, s0 - k0, 0.0))
    sums[2:8, :] = jnp.zeros((6, BW), f32)
    x_out[0] = (d + s0) - k0
    y_out[0] = s0 - 2.0 * d
    for t in range(1, NEAR):
        if t < 6:
            a = lax.rem(q + jnp.int32(offsets(0, nq)[t] + nq), jnp.int32(nq))
        else:
            step_3 = jnp.where(lax.rem(q, jnp.int32(2)) == 0, 3, nq - 3)
            a = lax.rem(q + step_3, jnp.int32(nq))
        m = mh[at(a), at(q)].astype(f32) + ml[at(a), at(q)].astype(f32)
        s = sq[at(a), :]
        x_out[t] = (m + s) - col[at(a), :]
        y_out[t] = s - 2.0 * m
    s0 = split(s0)
    for slot, cu, scu, part in cross:
        x_out[slot] = (cu + scu) - (dot3(*split(cu), *s0) + part)
        y_out[slot] = scu - 2.0 * cu


def finish_kernel(slots, lists, ids, parts, x_ref, y_ref, out_ref):
    sums = jnp.sum(parts[...], axis=0, keepdims=True)
    half = BW // 2
    low = jnp.broadcast_to(sums[:, 0:1], (1, BW))
    high = jnp.broadcast_to(sums[:, half : half + 1], (1, BW))
    c = high / low
    inv = 1.0 / (1.0 - c)
    own = lists[0, 0]
    for t in range(slots):
        a = lists[0, t]
        keep = jnp.logical_and(a >= 0, a <= own)
        out_ref[0, t] = jnp.where(keep, (x_ref[t] + c * y_ref[t]) * inv, 0.0)


def room(args, outs, scratch):
    sizes = [math.prod(a.shape) * a.dtype.itemsize for a in args]
    sizes += [math.prod(s) * jnp.dtype(d).itemsize for s, d in outs]
    sizes += [math.prod(s.shape) * jnp.dtype(s.dtype).itemsize for s in scratch]
    return min(sum(sizes) + SPARE, MOST)


def call(kernel, outs, args, scalars, scratch=(), flops=0):
    specs = [
        pl.BlockSpec(memory_space=pltpu.SMEM if i < scalars else pltpu.VMEM)
        for i in range(len(args))
    ]
    return pl.pallas_call(
        kernel,
        out_shape=[jax.ShapeDtypeStruct(s, d) for s, d in outs],
        in_specs=specs,
        out_specs=[pl.BlockSpec(memory_space=pltpu.VMEM) for _ in outs],
        scratch_shapes=list(scratch),
        compiler_params=pltpu.CompilerParams(vmem_limit_bytes=room(args, outs, scratch)),
        cost_estimate=pl.CostEstimate(flops=flops, bytes_accessed=0, transcendentals=0),
    )(*args)


def spread(x, axis, size):
    return [x] + [
        lax.ppermute(x, axis, [(i, i ^ k) for i in range(size)]) for k in range(1, size)
    ]


def gather_pairs(most, few, own_pack, ids, nq):
    half = nq // 2
    size = [len(slots) for slots in stored(nq)]
    far = lambda keep: [(i, nq - 1 - i) for i in range(nq) if keep(i)]
    all_in = lax.ppermute(most, "col", far(lambda i: i >= half and size[i] > SOME))
    some_in = lax.ppermute(
        most[: 8 + SOME * BW], "col", far(lambda i: i >= half and size[i] <= SOME)
    )
    few_in = lax.ppermute(few, "col", far(lambda i: i < half))
    pack_in = lax.ppermute(own_pack, "col", far(lambda i: True))
    front, back = call(
        functools.partial(pair_kernel, nq),
        [((HALF, BW), f32), ((TERMS + 2 * PACK - HALF, BW), f32)],
        (ids, most, all_in, some_in, few_in, own_pack, pack_in),
        1,
    )
    backs = tree_gather(back, "col", half, drop_high, nq // half)
    fronts = tree_gather(front, "col", half, drop_low, nq // half)
    return fronts + backs


def drop_low(m):
    return m & (m - 1)


def drop_high(m):
    return m ^ (1 << (m.bit_length() - 1))


def tree_gather(x, axis, size, parent, repeat=1):
    depth = lambda m: 0 if m == 0 else 1 + depth(parent(m))
    got = {0: x}
    for m in sorted(range(1, size), key=lambda m: (depth(m), -m)):
        step = m ^ parent(m)
        got[m] = lax.ppermute(got[parent(m)], axis, [(i, i ^ step) for i in range(size * repeat)])
    return [got[m] for m in range(size)]


def along(x, nq):
    return [x] + [
        lax.ppermute(x, "col", [(i, (i + 2 * k) % nq) for i in range(nq)])
        for k in range(1, nq // 2)
    ]


def across(parts, nq):
    return parts + [
        lax.ppermute(y, "col", [(i, i ^ 1) for i in range(nq)]) for y in parts
    ]


def body(upper_blocks, members):
    nr, nq = lax.axis_size("row"), lax.axis_size("col")
    blocks = upper_blocks[0]
    slots = blocks.shape[0]
    order = nq * BW
    npair = len(pattern(nq))
    ids = jnp.stack([lax.axis_index("row"), lax.axis_index("col")]).astype(jnp.int32)

    most, few, row_part = call(
        functools.partial(prepare_kernel, nq),
        [((8 + ALL * BW, BW), f32), ((8 + FEW * BW, BW), f32), ((3 * BW + 8, BW), f32)],
        (ids, members, blocks),
        2,
    )
    row = spread(row_part, "row", nr)
    lists = jnp.concatenate([x[3 * BW : 3 * BW + 1, :slots] for x in row]).astype(jnp.int32)

    square_flops = 6 * order**3
    listed = (npair, BW, BW)
    dense = (order, order)
    edges = (nr, BW, BW)
    pack = (PACK, BW)
    cross_outs = [(edges, f32)] * 4 + [(pack, f32)]
    square_outs = [(listed, f32), (dense, bf16), (dense, bf16), (pack, f32)]

    d, u, su, v, own = call(
        functools.partial(cross_first_kernel, nr, nq), cross_outs, (ids, lists, *row), 2,
        [pltpu.VMEM((nr, 3 * BW + 8, BW), f32)],
    )
    nears = gather_pairs(most, few, own, ids, nq)
    m, mh, ml, link, s, sh, sl, tell, packs = call(
        functools.partial(first_kernel, nq),
        [(listed, f32), (dense, bf16), (dense, bf16), ((nq, order), f32)]
        + square_outs
        + [((nq,) + pack, f32)],
        (ids, *nears, own),
        1,
        [pltpu.VMEM((nq // 2, TERMS + 2 * PACK, BW), f32)],
        flops=square_flops,
    )
    packs = [packs]
    for step in range(PURIFY - 1):
        rows = spread(tell, "row", nr)
        x, y = call(
            functools.partial(cube_kernel, nq),
            [(listed, f32)] * 2,
            (m, mh, ml, s, sh, sl, link),
            0,
            flops=square_flops,
        )
        if step == PURIFY - 2:
            break
        coef, d, u, su, v, own = call(
            functools.partial(cross_kernel, nr, nq, len(packs)),
            [((8, BW), f32)] + cross_outs,
            (ids, lists, *rows, *packs, d, u, su, v),
            2,
            [pltpu.VMEM((nq, 8, BW), f32), pltpu.VMEM((nr, PACK, BW), f32)],
            flops=square_flops // 4,
        )
        old = packs
        straight = along(own, nq)
        m, mh, ml, s, sh, sl, tell = call(
            functools.partial(next_kernel, nq, len(old)),
            [(listed, f32), (dense, bf16), (dense, bf16)] + square_outs,
            (ids, coef, *old, own, x, y, m, link),
            1,
            [pltpu.VMEM((nq, PACK, BW), f32)],
            flops=square_flops,
        )
        tell, *straight = lax.optimization_barrier((tell, *straight))
        packs = across(straight, nq)
    strip = (order, BW)
    xo, yo, sums = call(
        functools.partial(last_kernel, nr, nq, len(packs)),
        [((slots, BW, BW), f32)] * 2 + [((8, BW), f32)],
        (ids, lists, *rows, *packs, x, y, m, link, d, u, su, v),
        2,
        [
            pltpu.VMEM((nr, PACK, BW), f32),
            pltpu.VMEM((nq, 8, BW), f32),
            pltpu.VMEM((nq, PACK, BW), f32),
            pltpu.VMEM(listed, f32),
            pltpu.VMEM(dense, bf16),
            pltpu.VMEM(dense, bf16),
            pltpu.VMEM(strip, f32),
            pltpu.VMEM(strip, f32),
        ],
    )
    lane = jnp.arange(BW) < BW // 2
    mine = jnp.where(lane, sums[0], sums[1])
    parts = lax.all_to_all(
        jnp.broadcast_to(mine[None], (nr * nq, BW)), ("row", "col"), 0, 0, tiled=True
    )
    (out,) = call(
        functools.partial(finish_kernel, slots),
        [((1, slots, BW, BW), f32)],
        (lists, ids, parts, xo, yo),
        2,
    )
    return out


def solution(mesh):
    return jax.shard_map(
        body,
        mesh=mesh,
        in_specs=(P(("row", "col"), None, None, None), P(("row", "col"), None)),
        out_specs=P(("row", "col"), None, None, None),
        check_vma=False,
    )
```

```python
import functools
import math

import jax
import jax.numpy as jnp
from jax import lax
from jax.experimental import pallas as pl
from jax.experimental.pallas import tpu as pltpu
from jax.sharding import PartitionSpec as P

PURIFY = 3
BW = 128
TILE = 256
NEAR = 7
PACK = BW + 8
SPARE = 8 * 1024 * 1024
MOST = 60 * 1024 * 1024

f32 = jnp.float32
bf16 = jnp.bfloat16


def offsets(q, nq):
    return [0, -1, 1, -2, 2, nq // 2, 3 if q % 2 == 0 else -3]


@functools.lru_cache
def pattern(nq):
    pairs = [(q, q) for q in range(nq)]
    for b in range(nq):
        for d in offsets(b, nq)[1:]:
            a = (b + d) % nq
            if a < b:
                pairs.append((a, b))
    return tuple(pairs)


@functools.lru_cache
def pair_index(nq):
    return {pair: i for i, pair in enumerate(pattern(nq))}


def slot_of(a, b, nq):
    return [(b + d) % nq for d in offsets(b, nq)].index(a)


@functools.lru_cache
def tiles(nq):
    index = pair_index(nq)
    n = nq * BW // TILE
    per = TILE // BW

    def live(i, j):
        lo, hi = min(i, j), max(i, j)
        return any(
            (a, b) in index or (b, a) in index
            for a in range(lo * per, (lo + 1) * per)
            for b in range(hi * per, (hi + 1) * per)
        )

    out = []
    for i in range(n):
        for j in range(i, n):
            if live(i, j):
                inner = [k for k in range(n) if live(i, k) and live(k, j)]
                out.append((i, j, inner))
    return out


PAIR = 8
FEW, ALL = 4, 7
FRONT = 8 + FEW * BW
TERMS = FRONT + (PAIR - FEW) * BW + 8


@functools.lru_cache
def stored(nq):
    out = []
    for b in range(nq):
        out.append([t for t, d in enumerate(offsets(b, nq)) if (b + d) % nq <= b])
    for b in range(nq // 2):
        assert len(out[b]) <= FEW <= len(out[nq - 1 - b]) == PAIR - len(out[b])
    return out


def counts(nq):
    return [len(stored(nq)[nq - 1 - p]) for p in range(nq // 2)]


def pair_blocks(nq, p):
    return [
        ((b + offsets(b, nq)[t]) % nq, b) for b in (nq - 1 - p, p) for t in stored(nq)[b]
    ]


def split(x):
    hi = x.astype(bf16)
    return hi, (x - hi.astype(f32)).astype(bf16)


def mm(a, b):
    return jnp.dot(a, b, preferred_element_type=f32)


def dot3(ah, al, bh, bl):
    if bh.shape[1] != BW:
        return mm(ah, bh) + (mm(ah, bl) + mm(al, bh))
    if bh.shape[0] == BW:
        top = jnp.concatenate([bh, bl], axis=1)
        low = jnp.concatenate([bh, jnp.zeros_like(bl)], axis=1)
        both = mm(jnp.concatenate([ah, al], axis=1), jnp.concatenate([top, low], axis=0))
        return both[:, :BW] + both[:, BW:]
    both = mm(ah, jnp.concatenate([bh, bl], axis=1))
    return both[:, :BW] + (both[:, BW:] + mm(al, bh))


def dotf(a, b):
    return dot3(*split(a), *split(b))


def row_col():
    return (
        lax.broadcasted_iota(jnp.int32, (BW, BW), 0),
        lax.broadcasted_iota(jnp.int32, (BW, BW), 1),
    )


def total(x):
    s = jnp.sum(jnp.sum(x, axis=0, keepdims=True), axis=1, keepdims=True)
    return jnp.broadcast_to(s, (1, BW))


def pack_pair(ref, first, second):
    i, j = row_col()
    ref[0:BW, :] = jnp.where(i <= j, first, second)
    ref[BW : BW + 1, :] = jnp.sum(jnp.where(i == j, second, 0.0), axis=0, keepdims=True)


def unpack_pair(block, diagonal):
    i, j = row_col()
    flipped = block.T
    first = jnp.where(i <= j, block, flipped)
    second = jnp.where(i > j, block, jnp.where(i == j, diagonal, flipped))
    return first, second


def at(q):
    return pl.ds(pl.multiple_of(q * BW, BW), BW)


def cut(q):
    return slice(q * BW, (q + 1) * BW)


def settle(nq, q, parts, held, start=0, size=PACK):
    if len(parts) == 1:
        for k in range(nq):
            held[k] = parts[0][k, start : start + size, :]
        return
    half = nq // 2
    for k in range(half):
        held[q ^ (2 * k)] = parts[k][start : start + size, :]
        far = k * PACK + start
        held[q ^ (2 * k + 1)] = parts[half][far : far + size, :]


def put_dense(hi_ref, lo_ref, a, b, block):
    hi, lo = split(block)
    hi_ref[cut(a), cut(b)] = hi
    lo_ref[cut(a), cut(b)] = lo
    if a != b:
        hi, lo = split(block.T)
        hi_ref[cut(b), cut(a)] = hi
        lo_ref[cut(b), cut(a)] = lo


def clear_unlinked(hi_ref, lo_ref, nq):
    index = pair_index(nq)
    zero = jnp.zeros((BW, BW), bf16)
    for a in range(nq):
        for b in range(nq):
            if (min(a, b), max(a, b)) not in index:
                hi_ref[cut(a), cut(b)] = zero
                lo_ref[cut(a), cut(b)] = zero


def tile_products(ah, al, bh, bl, nq):
    index = pair_index(nq)
    per = TILE // BW
    n = nq * BW // TILE
    for i, j, inner in tiles(nq):
        rows, cols = slice(i * TILE, (i + 1) * TILE), slice(j * TILE, (j + 1) * TILE)
        if len(inner) == n:
            acc = dot3(ah[rows, :], al[rows, :], bh[:, cols], bl[:, cols])
        else:
            acc = None
            for k in inner:
                mid = slice(k * TILE, (k + 1) * TILE)
                part = dot3(ah[rows, mid], al[rows, mid], bh[mid, cols], bl[mid, cols])
                acc = part if acc is None else acc + part
        for x in range(per):
            for y in range(per):
                a, b = i * per + x, j * per + y
                if (a, b) in index:
                    yield (a, b), acc[cut(x), cut(y)]


def square_part(nq, q, own_pack, m_ref, mh, ml, link, s_ref, sh, sl, out_ref):
    index = pair_index(nq)
    clear_unlinked(sh, sl, nq)
    trace = jnp.zeros((BW, BW), f32)
    norm = jnp.zeros((BW, BW), f32)
    inner = jnp.zeros((BW, BW), f32)
    i, j = row_col()
    for (a, b), block in tile_products(mh, ml, mh, ml, nq):
        if a != b:
            block = block * link[a : a + 1, cut(b)]
        at_list = index[(a, b)]
        s_ref[at_list] = block
        put_dense(sh, sl, a, b, block)
        own = m_ref[at_list]
        if a == b:
            trace = trace + own
            norm = norm + own * own
            inner = inner + own * block
        else:
            norm = norm + 2.0 * (own * own)
            inner = inner + 2.0 * (own * block)
    g, e = unpack_pair(own_pack[0:BW, :], own_pack[BW : BW + 1, :])
    d = m_ref[q]
    dg = dotf(d, g)
    s0 = s_ref[q] + g
    k0 = dot3(mh[at(q), :], ml[at(q), :], sh[:, at(q)], sl[:, at(q)]) + (dg + dg.T) + e
    pack_pair(out_ref, s0, k0)
    out_ref[BW + 1 : BW + 2, :] = total(jnp.where(i == j, trace, 0.0))
    out_ref[BW + 2 : BW + 3, :] = total(norm)
    out_ref[BW + 3 : BW + 4, :] = total(inner)
    out_ref[BW + 4 : BW + 8, :] = jnp.zeros((4, BW), f32)


def choose(q, values):
    out = jnp.int32(values[0])
    for i, v in enumerate(values[1:], 1):
        if v != values[0]:
            out = jnp.where(q == i, jnp.int32(v), out)
    return out


def prepare_kernel(nq, names, blocks, few, rest, row):
    q = lax.axis_index("col")
    lists = names[...].astype(f32)
    for ref, start in ((few, 0), (row, 3 * BW)):
        ref[start : start + 8, :] = jnp.zeros((8, BW), f32)
        ref[start : start + 1, 0 : names.shape[1]] = lists
    for i in range(ALL):
        block = blocks[choose(q, [(slots + [0] * ALL)[i] for slots in stored(nq)])]
        if i < FEW:
            few[place(i), :] = block
        else:
            rest[cut(i - FEW), :] = block
    for i, t in enumerate((0, NEAR, NEAR + 1)):
        row[cut(i), :] = blocks[t]


def place(i):
    return slice(8 + i * BW, 8 + (i + 1) * BW)


def at_place(i):
    return pl.ds(pl.multiple_of(8 + i * BW, 8), BW)


def lay(i):
    return place(i) if i < FEW else cut_from(FRONT, i - FEW)


def cut_from(start, i):
    return slice(start + i * BW, start + (i + 1) * BW)


def back_kernel(nq, few, rest, few_in, rest_in, own_pack, pack_in, back):
    q = lax.axis_index("col")
    upper = q >= nq // 2
    count = choose(jnp.where(upper, nq - 1 - q, q), counts(nq)) - FEW

    def fill(first, second):
        for i in range(PAIR - FEW):
            if i < ALL - FEW:

                @pl.when(i < count)
                def _():
                    back[cut(i), :] = first[cut(i), :]

            @pl.when(i >= count)
            def _():
                back[cut(i), :] = second[at_place(i - count), :]

        end = (PAIR - FEW) * BW
        back[end : end + 8, :] = second[0:8, :]

    @pl.when(upper)
    def _():
        fill(rest, few_in)

    @pl.when(jnp.logical_not(upper))
    def _():
        fill(rest_in, few)

    terms = TERMS - FRONT
    back[terms : terms + PACK, :] = jnp.where(upper, own_pack[...], pack_in[...])
    back[terms + PACK :, :] = jnp.where(upper, pack_in[...], own_pack[...])


def first_kernel(nq, *refs):
    half = nq // 2
    fronts, backs, refs = refs[:half], refs[half:nq], refs[nq:]
    own_pack, m_ref, mh, ml, link, s_ref, sh, sl, out_ref, packs, near = refs
    q = lax.axis_index("col")
    own = jnp.minimum(q, nq - 1 - q)
    for m in range(half):
        near[m ^ own, 0:FRONT, :] = fronts[m][...]
        near[m ^ own, FRONT:, :] = backs[m][...]
    clear_unlinked(mh, ml, nq)
    link[...] = jnp.zeros_like(link)
    index = pair_index(nq)
    for p in range(half):
        packs[nq - 1 - p] = near[p, TERMS : TERMS + PACK, :]
        packs[p] = near[p, TERMS + PACK :, :]
        for i, pair in enumerate(pair_blocks(nq, p)):
            block = near[p, lay(i), :]
            m_ref[index[pair]] = block
            put_dense(mh, ml, *pair, block)
    for a in range(nq):
        row = 0 if a >= half else TERMS - 8
        listed = near[min(a, nq - 1 - a), row : row + 1, :]
        present = jnp.where(listed >= 0.0, 1.0, 0.0)
        for t, d in enumerate(offsets(a, nq)):
            b = (a + d) % nq
            link[a : a + 1, cut(b)] = jnp.broadcast_to(present[:, t : t + 1], (1, BW))
    square_part(nq, q, own_pack, m_ref, mh, ml, link, s_ref, sh, sl, out_ref)


def assemble(nq, q, c, inv, packs, x_ref, y_ref, m_old, held, m_ref, mh, ml):
    index = pair_index(nq)
    settle(nq, q, packs, held)
    clear_unlinked(mh, ml, nq)
    for b in range(nq):
        g, e = unpack_pair(held[b, 0:BW, :], held[b, BW : BW + 1, :])
        rows = [a for a in range(nq) if (a, b) in index]
        stack = jnp.concatenate([m_old[index[(a, b)]] for a in rows], axis=0)
        fixes = dotf(stack, g)
        for i, a in enumerate(rows):
            fix = fixes[cut(i), :]
            place = index[(a, b)]
            block = x_ref[place] + c * y_ref[place]
            if a == b:
                block = block + (1.0 + c) * g - (fix + fix.T + e)
            else:
                block = block - fix
            block = block * inv
            m_ref[place] = block
            put_dense(mh, ml, a, b, block)


def next_kernel(nq, count, coef, *refs):
    packs, own_pack, refs = refs[:count], refs[count], refs[count + 1 :]
    x_ref, y_ref, m_old, link, m_ref, mh, ml, s_ref, sh, sl, out_ref, held = refs
    q = lax.axis_index("col")
    assemble(nq, q, coef[0:1, :], coef[1:2, :], packs, x_ref, y_ref, m_old, held, m_ref, mh, ml)
    square_part(nq, q, own_pack, m_ref, mh, ml, link, s_ref, sh, sl, out_ref)


def cube_kernel(nq, m_ref, mh, ml, s_ref, sh, sl, link, x_ref, y_ref):
    index = pair_index(nq)
    for (a, b), block in tile_products(mh, ml, sh, sl, nq):
        if a != b:
            block = block * link[a : a + 1, cut(b)]
        place = index[(a, b)]
        m, s = m_ref[place], s_ref[place]
        x_ref[place] = (m + s) - block
        y_ref[place] = s - 2.0 * m


def far_row(lists, r, nq, e, slot):
    return lax.div(lists[e ^ r, slot], jnp.int32(nq))


def edge_ends(lists, r, nq, e):
    far = far_row(lists, r, nq, e, 8)
    return jnp.minimum(far, e), jnp.maximum(far, e)


def cross_tail(nr, nq, lists, d_ref, u_ref, su_ref, v_ref, pack_ref):
    r = lax.axis_index("row")
    norm = jnp.zeros((BW, BW), f32)
    inner = jnp.zeros((BW, BW), f32)
    for e in range(nr):
        lo, hi = edge_ends(lists, r, nq, e)
        u = u_ref[e]
        uh, ul = split(u)
        dlo = split(d_ref[lo])
        su = dot3(uh, ul, *split(d_ref[hi])) + dot3(*dlo, uh, ul)
        su_ref[e] = su
        v_ref[e] = dot3(*dlo, *split(su))
        norm = norm + u * u
        inner = inner + u * su
    g_sum = jnp.zeros((BW, BW), f32)
    e_sum = jnp.zeros((BW, BW), f32)
    for slot in (7, 8):
        far = far_row(lists, r, nq, r, slot)
        u = u_ref[r if slot == 8 else far]
        flipped = u.T
        mine = r > far
        cu = split(jnp.where(mine, u, flipped))
        cut_ = split(jnp.where(mine, flipped, u))
        g_sum = g_sum + dot3(*cut_, *cu)
        t = dot3(*split(d_ref[far]), *cu)
        e_sum = e_sum + dot3(*cut_, *split(t))
    pack_pair(pack_ref, g_sum, e_sum)
    pack_ref[BW + 1 : BW + 2, :] = 2.0 * total(norm)
    pack_ref[BW + 2 : BW + 3, :] = 3.0 * total(inner)
    pack_ref[BW + 3 : BW + 8, :] = jnp.zeros((5, BW), f32)


def cross_first_kernel(nr, nq, lists, *refs):
    parts, refs = refs[:nr], refs[nr:]
    d_ref, u_ref, su_ref, v_ref, pack_ref, row = refs
    r = lax.axis_index("row")
    for k in range(nr):
        row[k ^ r] = parts[k][...]
    for e in range(nr):
        d_ref[e] = row[e, cut(0), :]
    for e in range(nr):
        far = far_row(lists, r, nq, e, 8)
        here = row[e, cut(2), :]
        there = row[far, cut(1), :]
        u_ref[e] = jnp.where(far < e, here, there)
    cross_tail(nr, nq, lists, d_ref, u_ref, su_ref, v_ref, pack_ref)


def coefficient(nr, nq, q, rows, packs, held):
    settle(nq, q, packs, held, BW, 8)
    trace = rows[0, BW + 1 : BW + 2, :]
    norm = rows[0, BW + 2 : BW + 3, :]
    inner = rows[0, BW + 3 : BW + 4, :]
    for r in range(1, nr):
        trace = trace + rows[r, BW + 1 : BW + 2, :]
        norm = norm + rows[r, BW + 2 : BW + 3, :]
        inner = inner + rows[r, BW + 3 : BW + 4, :]
    for k in range(nq):
        norm = norm + held[k, 1:2, :]
        inner = inner + held[k, 2:3, :]
    c = (norm - inner) / (trace - norm)
    return c, 1.0 / (1.0 - c)


def cross_kernel(nr, nq, count, lists, *refs):
    parts, packs, refs = refs[:nr], refs[nr : nr + count], refs[nr + count :]
    d_old, u_old, su_old, v_old, coef, d_ref, u_ref, su_ref, v_ref, pack_ref, held, rows = refs
    r = lax.axis_index("row")
    for k in range(nr):
        rows[k ^ r] = parts[k][...]
    c, inv = coefficient(nr, nq, lax.axis_index("col"), rows, packs, held)
    coef[0:1, :] = c
    coef[1:2, :] = inv
    coef[2:8, :] = jnp.zeros((6, BW), f32)
    for p in range(nr):
        s0, k0 = unpack_pair(rows[p, 0:BW, :], rows[p, BW : BW + 1, :])
        d = d_old[p]
        d_ref[p] = ((1.0 - 2.0 * c) * d + (1.0 + c) * s0 - k0) * inv
    for e in range(nr):
        lo, hi = edge_ends(lists, r, nq, e)
        s0, _ = unpack_pair(rows[hi, 0:BW, :], rows[hi, BW : BW + 1, :])
        u, su = u_old[e], su_old[e]
        k = dotf(u, s0) + v_old[e]
        u_ref[e] = ((1.0 - 2.0 * c) * u + (1.0 + c) * su - k) * inv
    cross_tail(nr, nq, lists, d_ref, u_ref, su_ref, v_ref, pack_ref)


def last_kernel(nr, nq, count, lists, *refs):
    parts, packs, refs = refs[:nr], refs[nr : nr + count], refs[nr + count :]
    x_old, y_old, m_old, link, d_old, u_old, su_old, v_old = refs[:8]
    x_out, y_out, sums, rows, ends, held, m_ref, mh, ml, col, sq = refs[8:]
    r, q = lax.axis_index("row"), lax.axis_index("col")
    for k in range(nr):
        rows[k ^ r] = parts[k][...]
    c, inv = coefficient(nr, nq, q, rows, packs, ends)

    def step(p, s, k):
        return ((1.0 - 2.0 * c) * p + (1.0 + c) * s - k) * inv

    def told(p):
        return unpack_pair(rows[p, 0:BW, :], rows[p, BW : BW + 1, :])

    assemble(nq, q, c, inv, packs, x_old, y_old, m_old, held, m_ref, mh, ml)
    d = m_ref[q]
    g = jnp.zeros((BW, BW), f32)
    e = jnp.zeros((BW, BW), f32)
    cross = []
    for slot in (7, 8):
        far = far_row(lists, r, nq, r, slot)
        edge = r if slot == 8 else far
        u, su = u_old[edge], su_old[edge]
        u = step(u, su, dotf(u, told(jnp.maximum(far, r))[0]) + v_old[edge])
        flipped = u.T
        mine = r > far
        cu = jnp.where(mine, u, flipped)
        cut_ = split(jnp.where(mine, flipped, u))
        far_d = split(step(d_old[far], *told(far)))
        t = dot3(*far_d, *split(cu))
        scu = dotf(cu, d) + t
        g = g + dot3(*cut_, *split(cu))
        e = e + dot3(*cut_, *split(t))
        cross.append((slot, cu, scu, dot3(*far_d, *split(scu))))
    sq[...] = dot3(mh[...], ml[...], mh[:, at(q)], ml[:, at(q)])
    for a in range(nq):
        sq[cut(a), :] = sq[cut(a), :] * link[a : a + 1, at(q)]
    sq[at(q), :] = sq[at(q), :] + g
    col[...] = dot3(mh[...], ml[...], *split(sq[...]))
    s0 = sq[at(q), :]
    k0 = col[at(q), :] + dotf(g, d) + e
    i, j = row_col()
    sums[0:1, :] = total(jnp.where(i == j, d - s0, 0.0))
    sums[1:2, :] = total(jnp.where(i == j, s0 - k0, 0.0))
    sums[2:8, :] = jnp.zeros((6, BW), f32)

    def put(t, p, s, k):
        keep = jnp.logical_and(lists[0, t] >= 0, lists[0, t] <= lists[0, 0])
        x_out[t] = jnp.where(keep, (p + s) - k, 0.0)
        y_out[t] = jnp.where(keep, s - 2.0 * p, 0.0)

    put(0, d, s0, k0)
    for t in range(1, NEAR):
        if t < 6:
            a = lax.rem(q + jnp.int32(offsets(0, nq)[t] + nq), jnp.int32(nq))
        else:
            step_3 = jnp.where(lax.rem(q, jnp.int32(2)) == 0, 3, nq - 3)
            a = lax.rem(q + step_3, jnp.int32(nq))
        m = mh[at(a), at(q)].astype(f32) + ml[at(a), at(q)].astype(f32)
        put(t, m, sq[at(a), :], col[at(a), :])
    s0 = split(s0)
    for slot, cu, scu, part in cross:
        put(slot, cu, scu, dot3(*split(cu), *s0) + part)


def finish_kernel(slots, parts, x_ref, y_ref, out_ref):
    sums = jnp.sum(parts[...], axis=0, keepdims=True)
    half = BW // 2
    low = jnp.broadcast_to(sums[:, 0:1], (1, BW))
    high = jnp.broadcast_to(sums[:, half : half + 1], (1, BW))
    c = high / low
    inv = 1.0 / (1.0 - c)
    for t in range(slots):
        out_ref[0, t] = (x_ref[t] + c * y_ref[t]) * inv


def room(args, outs, scratch):
    sizes = [math.prod(a.shape) * a.dtype.itemsize for a in args]
    sizes += [math.prod(s) * jnp.dtype(d).itemsize for s, d in outs]
    sizes += [math.prod(s.shape) * jnp.dtype(s.dtype).itemsize for s in scratch]
    return min(sum(sizes) + SPARE, MOST)


def call(kernel, outs, args, scalars, scratch=(), flops=0):
    specs = [
        pl.BlockSpec(memory_space=pltpu.SMEM if i < scalars else pltpu.VMEM)
        for i in range(len(args))
    ]
    return pl.pallas_call(
        kernel,
        out_shape=[jax.ShapeDtypeStruct(s, d) for s, d in outs],
        in_specs=specs,
        out_specs=[pl.BlockSpec(memory_space=pltpu.VMEM) for _ in outs],
        scratch_shapes=list(scratch),
        compiler_params=pltpu.CompilerParams(vmem_limit_bytes=room(args, outs, scratch)),
        cost_estimate=pl.CostEstimate(flops=flops, bytes_accessed=0, transcendentals=0),
    )(*args)


def spread(x, axis, size):
    return [x] + [
        lax.ppermute(x, axis, [(i, i ^ k) for i in range(size)]) for k in range(1, size)
    ]


def gather_pairs(few, rest, own_pack, nq):
    half = nq // 2
    more = [len(slots) > FEW for slots in stored(nq)]
    mirror = [(i, nq - 1 - i) for i in range(nq)]
    few_in = lax.ppermute(few, "col", mirror)
    rest_in = lax.ppermute(rest, "col", [pair for pair in mirror if more[pair[0]]])
    pack_in = lax.ppermute(own_pack, "col", mirror)
    front = jnp.where(lax.axis_index("col") >= half, few, few_in)
    fronts = tree_gather(front, "col", half, drop_low, 2, levels=1)
    rest_in, fronts = lax.optimization_barrier((rest_in, fronts))
    (back,) = call(
        functools.partial(back_kernel, nq),
        [((TERMS + 2 * PACK - FRONT, BW), f32)],
        (few, rest, few_in, rest_in, own_pack, pack_in),
        0,
    )
    backs = tree_gather(back, "col", half, drop_high, 2)
    fronts = tree_gather(front, "col", half, drop_low, 2, fronts)
    return [got[m] for got in (fronts, backs) for m in range(half)]


def drop_low(m):
    return m & (m - 1)


def drop_high(m):
    return m ^ (1 << (m.bit_length() - 1))


def tree_gather(x, axis, size, parent, repeat=1, got=None, levels=8):
    depth = lambda m: 0 if m == 0 else 1 + depth(parent(m))
    got = dict(got or {0: x})
    for m in sorted(range(1, size), key=lambda m: (depth(m), -m)):
        if m in got or depth(m) > levels:
            continue
        step = m ^ parent(m)
        got[m] = lax.ppermute(got[parent(m)], axis, [(i, i ^ step) for i in range(size * repeat)])
    return got


def along(x, nq):
    return [x] + [
        lax.ppermute(x, "col", [(i, i ^ (2 * k)) for i in range(nq)]) for k in range(1, nq // 2)
    ]


def across(parts, nq):
    joined = jnp.concatenate(parts)
    return parts + [lax.ppermute(joined, "col", [(i, i ^ 1) for i in range(nq)])]


def body(upper_blocks, members):
    nr, nq = lax.axis_size("row"), lax.axis_size("col")
    blocks = upper_blocks[0]
    slots = blocks.shape[0]
    order = nq * BW
    npair = len(pattern(nq))

    few, rest, row_part = call(
        functools.partial(prepare_kernel, nq),
        [((FRONT, BW), f32), (((ALL - FEW) * BW, BW), f32), ((3 * BW + 8, BW), f32)],
        (members, blocks),
        0,
    )
    row = spread(row_part, "row", nr)
    lists = jnp.concatenate([x[3 * BW : 3 * BW + 1, :slots] for x in row]).astype(jnp.int32)

    square_flops = 6 * order**3
    listed = (npair, BW, BW)
    dense = (order, order)
    edges = (nr, BW, BW)
    pack = (PACK, BW)
    cross_outs = [(edges, f32)] * 4 + [(pack, f32)]
    square_outs = [(listed, f32), (dense, bf16), (dense, bf16), (pack, f32)]

    d, u, su, v, own = call(
        functools.partial(cross_first_kernel, nr, nq), cross_outs, (lists, *row), 1,
        [pltpu.VMEM((nr, 3 * BW + 8, BW), f32)],
    )
    nears = gather_pairs(few, rest, own, nq)
    m, mh, ml, link, s, sh, sl, tell, packs = call(
        functools.partial(first_kernel, nq),
        [(listed, f32), (dense, bf16), (dense, bf16), ((nq, order), f32)]
        + square_outs
        + [((nq,) + pack, f32)],
        (*nears, own),
        0,
        [pltpu.VMEM((nq // 2, TERMS + 2 * PACK, BW), f32)],
        flops=square_flops,
    )
    packs = [packs]
    rows = spread(tell, "row", nr)
    for step in range(PURIFY - 1):
        x, y = call(
            functools.partial(cube_kernel, nq),
            [(listed, f32)] * 2,
            (m, mh, ml, s, sh, sl, link),
            0,
            flops=square_flops,
        )
        if step == PURIFY - 2:
            break
        coef, d, u, su, v, own = call(
            functools.partial(cross_kernel, nr, nq, len(packs)),
            [((8, BW), f32)] + cross_outs,
            (lists, *rows, *packs, d, u, su, v),
            1,
            [pltpu.VMEM((nq, 8, BW), f32), pltpu.VMEM((nr, PACK, BW), f32)],
            flops=square_flops // 4,
        )
        old = packs
        straight = along(own, nq)
        m, mh, ml, s, sh, sl, tell = call(
            functools.partial(next_kernel, nq, len(old)),
            [(listed, f32), (dense, bf16), (dense, bf16)] + square_outs,
            (coef, *old, own, x, y, m, link),
            0,
            [pltpu.VMEM((nq, PACK, BW), f32)],
            flops=square_flops,
        )
        tell, *straight = lax.optimization_barrier((tell, *straight))
        rows = spread(tell, "row", nr)
        packs = across(straight, nq)
    strip = (order, BW)
    xo, yo, sums = call(
        functools.partial(last_kernel, nr, nq, len(packs)),
        [((slots, BW, BW), f32)] * 2 + [((8, BW), f32)],
        (lists, *rows, *packs, x, y, m, link, d, u, su, v),
        1,
        [
            pltpu.VMEM((nr, PACK, BW), f32),
            pltpu.VMEM((nq, 8, BW), f32),
            pltpu.VMEM((nq, PACK, BW), f32),
            pltpu.VMEM(listed, f32),
            pltpu.VMEM(dense, bf16),
            pltpu.VMEM(dense, bf16),
            pltpu.VMEM(strip, f32),
            pltpu.VMEM(strip, f32),
        ],
    )
    lane = jnp.arange(BW) < BW // 2
    mine = jnp.where(lane, sums[0], sums[1])
    parts = lax.all_to_all(
        jnp.broadcast_to(mine[None], (nr * nq, BW)), ("row", "col"), 0, 0, tiled=True
    )
    (out,) = call(
        functools.partial(finish_kernel, slots),
        [((1, slots, BW, BW), f32)],
        (parts, xo, yo),
        0,
    )
    return out


def solution(mesh):
    return jax.shard_map(
        body,
        mesh=mesh,
        in_specs=(P(("row", "col"), None, None, None), P(("row", "col"), None)),
        out_specs=P(("row", "col"), None, None, None),
        check_vma=False,
    )
```

```python
import functools
import math

import jax
import jax.numpy as jnp
from jax import lax
from jax.experimental import pallas as pl
from jax.experimental.pallas import tpu as pltpu
from jax.sharding import PartitionSpec as P

PURIFY = 3
BW = 128
TILE = 256
NEAR = 7
PACK = BW + 8
SPARE = 8 * 1024 * 1024
MOST = 60 * 1024 * 1024

f32 = jnp.float32
bf16 = jnp.bfloat16


def offsets(q, nq):
    return [0, -1, 1, -2, 2, nq // 2, 3 if q % 2 == 0 else -3]


@functools.lru_cache
def pattern(nq):
    pairs = [(q, q) for q in range(nq)]
    for b in range(nq):
        for d in offsets(b, nq)[1:]:
            a = (b + d) % nq
            if a < b:
                pairs.append((a, b))
    return tuple(pairs)


@functools.lru_cache
def pair_index(nq):
    return {pair: i for i, pair in enumerate(pattern(nq))}


def slot_of(a, b, nq):
    return [(b + d) % nq for d in offsets(b, nq)].index(a)


@functools.lru_cache
def tiles(nq):
    index = pair_index(nq)
    n = nq * BW // TILE
    per = TILE // BW

    def live(i, j):
        lo, hi = min(i, j), max(i, j)
        return any(
            (a, b) in index or (b, a) in index
            for a in range(lo * per, (lo + 1) * per)
            for b in range(hi * per, (hi + 1) * per)
        )

    out = []
    for i in range(n):
        for j in range(i, n):
            if live(i, j):
                inner = [k for k in range(n) if live(i, k) and live(k, j)]
                out.append((i, j, inner))
    return out


PAIR = 8
FEW, ALL = 4, 7
FRONT = 8 + FEW * BW
TERMS = FRONT + (PAIR - FEW) * BW + 8


@functools.lru_cache
def stored(nq):
    out = []
    for b in range(nq):
        out.append([t for t, d in enumerate(offsets(b, nq)) if (b + d) % nq <= b])
    for b in range(nq // 2):
        assert len(out[b]) <= FEW <= len(out[nq - 1 - b]) == PAIR - len(out[b])
    return out


def counts(nq):
    return [len(stored(nq)[nq - 1 - p]) for p in range(nq // 2)]


def pair_blocks(nq, p):
    return [
        ((b + offsets(b, nq)[t]) % nq, b) for b in (nq - 1 - p, p) for t in stored(nq)[b]
    ]


def split(x):
    hi = x.astype(bf16)
    return hi, (x - hi.astype(f32)).astype(bf16)


def mm(a, b):
    return jnp.dot(a, b, preferred_element_type=f32)


def dot3(ah, al, bh, bl):
    if bh.shape[1] != BW:
        return mm(ah, bh) + (mm(ah, bl) + mm(al, bh))
    if bh.shape[0] == BW:
        top = jnp.concatenate([bh, bl], axis=1)
        low = jnp.concatenate([bh, jnp.zeros_like(bl)], axis=1)
        both = mm(jnp.concatenate([ah, al], axis=1), jnp.concatenate([top, low], axis=0))
        return both[:, :BW] + both[:, BW:]
    both = mm(ah, jnp.concatenate([bh, bl], axis=1))
    return both[:, :BW] + (both[:, BW:] + mm(al, bh))


def dotf(a, b):
    return dot3(*split(a), *split(b))


def row_col():
    return (
        lax.broadcasted_iota(jnp.int32, (BW, BW), 0),
        lax.broadcasted_iota(jnp.int32, (BW, BW), 1),
    )


def total(x):
    s = jnp.sum(jnp.sum(x, axis=0, keepdims=True), axis=1, keepdims=True)
    return jnp.broadcast_to(s, (1, BW))


def pack_pair(ref, first, second):
    i, j = row_col()
    ref[0:BW, :] = jnp.where(i <= j, first, second)
    ref[BW : BW + 1, :] = jnp.sum(jnp.where(i == j, second, 0.0), axis=0, keepdims=True)


def unpack_pair(block, diagonal):
    i, j = row_col()
    flipped = block.T
    first = jnp.where(i <= j, block, flipped)
    second = jnp.where(i > j, block, jnp.where(i == j, diagonal, flipped))
    return first, second


def at(q):
    return pl.ds(pl.multiple_of(q * BW, BW), BW)


def cut(q):
    return slice(q * BW, (q + 1) * BW)


def settle(nq, q, parts, held, start=0, size=PACK):
    if len(parts) == 1:
        for k in range(nq):
            held[k] = parts[0][k, start : start + size, :]
        return
    half = nq // 2
    for k in range(half):
        held[q ^ (2 * k)] = parts[k][start : start + size, :]
        far = k * PACK + start
        held[q ^ (2 * k + 1)] = parts[half][far : far + size, :]


def put_dense(hi_ref, lo_ref, a, b, block):
    hi, lo = split(block)
    hi_ref[cut(a), cut(b)] = hi
    lo_ref[cut(a), cut(b)] = lo
    if a != b:
        hi, lo = split(block.T)
        hi_ref[cut(b), cut(a)] = hi
        lo_ref[cut(b), cut(a)] = lo


def clear_unlinked(hi_ref, lo_ref, nq):
    index = pair_index(nq)
    zero = jnp.zeros((BW, BW), bf16)
    for a in range(nq):
        for b in range(nq):
            if (min(a, b), max(a, b)) not in index:
                hi_ref[cut(a), cut(b)] = zero
                lo_ref[cut(a), cut(b)] = zero


def tile_products(ah, al, bh, bl, nq):
    index = pair_index(nq)
    per = TILE // BW
    n = nq * BW // TILE
    for i, j, inner in tiles(nq):
        rows, cols = slice(i * TILE, (i + 1) * TILE), slice(j * TILE, (j + 1) * TILE)
        if len(inner) == n:
            acc = dot3(ah[rows, :], al[rows, :], bh[:, cols], bl[:, cols])
        else:
            acc = None
            for k in inner:
                mid = slice(k * TILE, (k + 1) * TILE)
                part = dot3(ah[rows, mid], al[rows, mid], bh[mid, cols], bl[mid, cols])
                acc = part if acc is None else acc + part
        for x in range(per):
            for y in range(per):
                a, b = i * per + x, j * per + y
                if (a, b) in index:
                    yield (a, b), acc[cut(x), cut(y)]


def square_part(nq, q, own_pack, m_ref, mh, ml, link, s_ref, sh, sl, out_ref):
    index = pair_index(nq)
    clear_unlinked(sh, sl, nq)
    trace = jnp.zeros((BW, BW), f32)
    norm = jnp.zeros((BW, BW), f32)
    inner = jnp.zeros((BW, BW), f32)
    i, j = row_col()
    for (a, b), block in tile_products(mh, ml, mh, ml, nq):
        if a != b:
            block = block * link[a : a + 1, cut(b)]
        at_list = index[(a, b)]
        s_ref[at_list] = block
        put_dense(sh, sl, a, b, block)
        own = m_ref[at_list]
        if a == b:
            trace = trace + own
            norm = norm + own * own
            inner = inner + own * block
        else:
            norm = norm + 2.0 * (own * own)
            inner = inner + 2.0 * (own * block)
    g, e = unpack_pair(own_pack[0:BW, :], own_pack[BW : BW + 1, :])
    d = m_ref[q]
    dg = dotf(d, g)
    s0 = s_ref[q] + g
    k0 = dot3(mh[at(q), :], ml[at(q), :], sh[:, at(q)], sl[:, at(q)]) + (dg + dg.T) + e
    pack_pair(out_ref, s0, k0)
    out_ref[BW + 1 : BW + 2, :] = total(jnp.where(i == j, trace, 0.0))
    out_ref[BW + 2 : BW + 3, :] = total(norm)
    out_ref[BW + 3 : BW + 4, :] = total(inner)
    out_ref[BW + 4 : BW + 8, :] = jnp.zeros((4, BW), f32)


def choose(q, values):
    out = jnp.int32(values[0])
    for i, v in enumerate(values[1:], 1):
        if v != values[0]:
            out = jnp.where(q == i, jnp.int32(v), out)
    return out


def prepare_kernel(nq, names, blocks, few, rest, row):
    q = lax.axis_index("col")
    lists = names[...].astype(f32)
    for ref, start in ((few, 0), (row, 3 * BW)):
        ref[start : start + 8, :] = jnp.zeros((8, BW), f32)
        ref[start : start + 1, 0 : names.shape[1]] = lists
    for i in range(ALL):
        block = blocks[choose(q, [(slots + [0] * ALL)[i] for slots in stored(nq)])]
        if i < FEW:
            few[place(i), :] = block
        else:
            rest[cut(i - FEW), :] = block
    for i, t in enumerate((0, NEAR, NEAR + 1)):
        row[cut(i), :] = blocks[t]


def place(i):
    return slice(8 + i * BW, 8 + (i + 1) * BW)


def at_place(i):
    return pl.ds(pl.multiple_of(8 + i * BW, 8), BW)


def lay(i):
    return place(i) if i < FEW else cut_from(FRONT, i - FEW)


def cut_from(start, i):
    return slice(start + i * BW, start + (i + 1) * BW)


def back_kernel(nq, few, rest, few_in, rest_in, own_pack, pack_in, back):
    q = lax.axis_index("col")
    upper = q >= nq // 2
    count = choose(jnp.where(upper, nq - 1 - q, q), counts(nq)) - FEW

    def fill(first, second):
        for i in range(PAIR - FEW):
            if i < ALL - FEW:

                @pl.when(i < count)
                def _():
                    back[cut(i), :] = first[cut(i), :]

            @pl.when(i >= count)
            def _():
                back[cut(i), :] = second[at_place(i - count), :]

        end = (PAIR - FEW) * BW
        back[end : end + 8, :] = second[0:8, :]

    @pl.when(upper)
    def _():
        fill(rest, few_in)

    @pl.when(jnp.logical_not(upper))
    def _():
        fill(rest_in, few)

    terms = TERMS - FRONT
    back[terms : terms + PACK, :] = jnp.where(upper, own_pack[...], pack_in[...])
    back[terms + PACK :, :] = jnp.where(upper, pack_in[...], own_pack[...])


def first_kernel(nq, *refs):
    half = nq // 2
    fronts, backs, refs = refs[:half], refs[half:nq], refs[nq:]
    own_pack, m_ref, mh, ml, link, s_ref, sh, sl, out_ref, packs, near = refs
    q = lax.axis_index("col")
    own = jnp.minimum(q, nq - 1 - q)
    for m in range(half):
        near[m ^ own, 0:FRONT, :] = fronts[m][...]
        near[m ^ own, FRONT:, :] = backs[m][...]
    clear_unlinked(mh, ml, nq)
    link[...] = jnp.zeros_like(link)
    index = pair_index(nq)
    for p in range(half):
        packs[nq - 1 - p] = near[p, TERMS : TERMS + PACK, :]
        packs[p] = near[p, TERMS + PACK :, :]
        for i, pair in enumerate(pair_blocks(nq, p)):
            block = near[p, lay(i), :]
            m_ref[index[pair]] = block
            put_dense(mh, ml, *pair, block)
    for a in range(nq):
        row = 0 if a >= half else TERMS - 8
        listed = near[min(a, nq - 1 - a), row : row + 1, :]
        present = jnp.where(listed >= 0.0, 1.0, 0.0)
        for t, d in enumerate(offsets(a, nq)):
            b = (a + d) % nq
            link[a : a + 1, cut(b)] = jnp.broadcast_to(present[:, t : t + 1], (1, BW))
    square_part(nq, q, own_pack, m_ref, mh, ml, link, s_ref, sh, sl, out_ref)


def assemble(nq, q, c, inv, packs, x_ref, y_ref, m_old, held, m_ref, mh, ml):
    index = pair_index(nq)
    settle(nq, q, packs, held)
    clear_unlinked(mh, ml, nq)
    for b in range(nq):
        g, e = unpack_pair(held[b, 0:BW, :], held[b, BW : BW + 1, :])
        rows = [a for a in range(nq) if (a, b) in index]
        stack = jnp.concatenate([m_old[index[(a, b)]] for a in rows], axis=0)
        fixes = dotf(stack, g)
        for i, a in enumerate(rows):
            fix = fixes[cut(i), :]
            place = index[(a, b)]
            block = x_ref[place] + c * y_ref[place]
            if a == b:
                block = block + (1.0 + c) * g - (fix + fix.T + e)
            else:
                block = block - fix
            block = block * inv
            m_ref[place] = block
            put_dense(mh, ml, a, b, block)


def next_kernel(nq, count, coef, *refs):
    packs, own_pack, refs = refs[:count], refs[count], refs[count + 1 :]
    x_ref, y_ref, m_old, link, m_ref, mh, ml, s_ref, sh, sl, out_ref, held = refs
    q = lax.axis_index("col")
    assemble(nq, q, coef[0:1, :], coef[1:2, :], packs, x_ref, y_ref, m_old, held, m_ref, mh, ml)
    square_part(nq, q, own_pack, m_ref, mh, ml, link, s_ref, sh, sl, out_ref)


def cube_kernel(nq, m_ref, mh, ml, s_ref, sh, sl, link, x_ref, y_ref):
    index = pair_index(nq)
    for (a, b), block in tile_products(mh, ml, sh, sl, nq):
        if a != b:
            block = block * link[a : a + 1, cut(b)]
        place = index[(a, b)]
        m, s = m_ref[place], s_ref[place]
        x_ref[place] = (m + s) - block
        y_ref[place] = s - 2.0 * m


def far_row(lists, r, nq, e, slot):
    return lax.div(lists[e ^ r, slot], jnp.int32(nq))


def edge_ends(lists, r, nq, e):
    far = far_row(lists, r, nq, e, 8)
    return jnp.minimum(far, e), jnp.maximum(far, e)


def cross_tail(nr, nq, lists, d_ref, u_ref, su_ref, v_ref, pack_ref):
    r = lax.axis_index("row")
    norm = jnp.zeros((BW, BW), f32)
    inner = jnp.zeros((BW, BW), f32)
    for e in range(nr):
        lo, hi = edge_ends(lists, r, nq, e)
        u = u_ref[e]
        uh, ul = split(u)
        dlo = split(d_ref[lo])
        su = dot3(uh, ul, *split(d_ref[hi])) + dot3(*dlo, uh, ul)
        su_ref[e] = su
        v_ref[e] = dot3(*dlo, *split(su))
        norm = norm + u * u
        inner = inner + u * su
    g_sum = jnp.zeros((BW, BW), f32)
    e_sum = jnp.zeros((BW, BW), f32)
    for slot in (7, 8):
        far = far_row(lists, r, nq, r, slot)
        u = u_ref[r if slot == 8 else far]
        flipped = u.T
        mine = r > far
        cu = split(jnp.where(mine, u, flipped))
        cut_ = split(jnp.where(mine, flipped, u))
        g_sum = g_sum + dot3(*cut_, *cu)
        t = dot3(*split(d_ref[far]), *cu)
        e_sum = e_sum + dot3(*cut_, *split(t))
    pack_pair(pack_ref, g_sum, e_sum)
    pack_ref[BW + 1 : BW + 2, :] = 2.0 * total(norm)
    pack_ref[BW + 2 : BW + 3, :] = 3.0 * total(inner)
    pack_ref[BW + 3 : BW + 8, :] = jnp.zeros((5, BW), f32)


def cross_first_kernel(nr, nq, lists, *refs):
    parts, refs = refs[:nr], refs[nr:]
    d_ref, u_ref, su_ref, v_ref, pack_ref, row = refs
    r = lax.axis_index("row")
    for k in range(nr):
        row[k ^ r] = parts[k][...]
    for e in range(nr):
        d_ref[e] = row[e, cut(0), :]
    for e in range(nr):
        far = far_row(lists, r, nq, e, 8)
        here = row[e, cut(2), :]
        there = row[far, cut(1), :]
        u_ref[e] = jnp.where(far < e, here, there)
    cross_tail(nr, nq, lists, d_ref, u_ref, su_ref, v_ref, pack_ref)


def coefficient(nr, nq, q, rows, packs, held):
    settle(nq, q, packs, held, BW, 8)
    trace = rows[0, BW + 1 : BW + 2, :]
    norm = rows[0, BW + 2 : BW + 3, :]
    inner = rows[0, BW + 3 : BW + 4, :]
    for r in range(1, nr):
        trace = trace + rows[r, BW + 1 : BW + 2, :]
        norm = norm + rows[r, BW + 2 : BW + 3, :]
        inner = inner + rows[r, BW + 3 : BW + 4, :]
    for k in range(nq):
        norm = norm + held[k, 1:2, :]
        inner = inner + held[k, 2:3, :]
    c = (norm - inner) / (trace - norm)
    return c, 1.0 / (1.0 - c)


def cross_kernel(nr, nq, count, lists, *refs):
    parts, packs, refs = refs[:nr], refs[nr : nr + count], refs[nr + count :]
    d_old, u_old, su_old, v_old, coef, d_ref, u_ref, su_ref, v_ref, pack_ref, held, rows = refs
    r = lax.axis_index("row")
    for k in range(nr):
        rows[k ^ r] = parts[k][...]
    c, inv = coefficient(nr, nq, lax.axis_index("col"), rows, packs, held)
    coef[0:1, :] = c
    coef[1:2, :] = inv
    coef[2:8, :] = jnp.zeros((6, BW), f32)
    for p in range(nr):
        s0, k0 = unpack_pair(rows[p, 0:BW, :], rows[p, BW : BW + 1, :])
        d = d_old[p]
        d_ref[p] = ((1.0 - 2.0 * c) * d + (1.0 + c) * s0 - k0) * inv
    for e in range(nr):
        lo, hi = edge_ends(lists, r, nq, e)
        s0, _ = unpack_pair(rows[hi, 0:BW, :], rows[hi, BW : BW + 1, :])
        u, su = u_old[e], su_old[e]
        k = dotf(u, s0) + v_old[e]
        u_ref[e] = ((1.0 - 2.0 * c) * u + (1.0 + c) * su - k) * inv
    cross_tail(nr, nq, lists, d_ref, u_ref, su_ref, v_ref, pack_ref)


def last_kernel(nr, nq, count, lists, *refs):
    parts, packs, refs = refs[:nr], refs[nr : nr + count], refs[nr + count :]
    x_old, y_old, m_old, link, d_old, u_old, su_old, v_old = refs[:8]
    x_out, y_out, sums, rows, ends, held, m_ref, mh, ml, col, sq = refs[8:]
    r, q = lax.axis_index("row"), lax.axis_index("col")
    for k in range(nr):
        rows[k ^ r] = parts[k][...]
    c, inv = coefficient(nr, nq, q, rows, packs, ends)

    def step(p, s, k):
        return ((1.0 - 2.0 * c) * p + (1.0 + c) * s - k) * inv

    def told(p):
        return unpack_pair(rows[p, 0:BW, :], rows[p, BW : BW + 1, :])

    assemble(nq, q, c, inv, packs, x_old, y_old, m_old, held, m_ref, mh, ml)
    d = m_ref[q]
    g = jnp.zeros((BW, BW), f32)
    e = jnp.zeros((BW, BW), f32)
    cross = []
    for slot in (7, 8):
        far = far_row(lists, r, nq, r, slot)
        edge = r if slot == 8 else far
        u, su = u_old[edge], su_old[edge]
        u = step(u, su, dotf(u, told(jnp.maximum(far, r))[0]) + v_old[edge])
        flipped = u.T
        mine = r > far
        cu = jnp.where(mine, u, flipped)
        cut_ = split(jnp.where(mine, flipped, u))
        far_d = split(step(d_old[far], *told(far)))
        t = dot3(*far_d, *split(cu))
        scu = dotf(cu, d) + t
        g = g + dot3(*cut_, *split(cu))
        e = e + dot3(*cut_, *split(t))
        cross.append((slot, cu, scu, dot3(*far_d, *split(scu))))
    sq[...] = dot3(mh[...], ml[...], mh[:, at(q)], ml[:, at(q)])
    for a in range(nq):
        sq[cut(a), :] = sq[cut(a), :] * link[a : a + 1, at(q)]
    sq[at(q), :] = sq[at(q), :] + g
    col[...] = dot3(mh[...], ml[...], *split(sq[...]))
    s0 = sq[at(q), :]
    k0 = col[at(q), :] + dotf(g, d) + e
    i, j = row_col()
    sums[0:1, :] = total(jnp.where(i == j, d - s0, 0.0))
    sums[1:2, :] = total(jnp.where(i == j, s0 - k0, 0.0))
    sums[2:8, :] = jnp.zeros((6, BW), f32)

    def put(t, p, s, k):
        keep = jnp.logical_and(lists[0, t] >= 0, lists[0, t] <= lists[0, 0])
        x_out[t] = jnp.where(keep, (p + s) - k, 0.0)
        y_out[t] = jnp.where(keep, s - 2.0 * p, 0.0)

    put(0, d, s0, k0)
    for t in range(1, NEAR):
        if t < 6:
            a = lax.rem(q + jnp.int32(offsets(0, nq)[t] + nq), jnp.int32(nq))
        else:
            step_3 = jnp.where(lax.rem(q, jnp.int32(2)) == 0, 3, nq - 3)
            a = lax.rem(q + step_3, jnp.int32(nq))
        m = mh[at(a), at(q)].astype(f32) + ml[at(a), at(q)].astype(f32)
        put(t, m, sq[at(a), :], col[at(a), :])
    s0 = split(s0)
    for slot, cu, scu, part in cross:
        put(slot, cu, scu, dot3(*split(cu), *s0) + part)


def finish_kernel(slots, parts, x_ref, y_ref, out_ref):
    sums = jnp.sum(parts[...], axis=0, keepdims=True)
    half = BW // 2
    low = jnp.broadcast_to(sums[:, 0:1], (1, BW))
    high = jnp.broadcast_to(sums[:, half : half + 1], (1, BW))
    c = high / low
    inv = 1.0 / (1.0 - c)
    for t in range(slots):
        out_ref[0, t] = (x_ref[t] + c * y_ref[t]) * inv


def room(args, outs, scratch):
    sizes = [math.prod(a.shape) * a.dtype.itemsize for a in args]
    sizes += [math.prod(s) * jnp.dtype(d).itemsize for s, d in outs]
    sizes += [math.prod(s.shape) * jnp.dtype(s.dtype).itemsize for s in scratch]
    return min(sum(sizes) + SPARE, MOST)


def call(kernel, outs, args, scalars, scratch=(), flops=0):
    specs = [
        pl.BlockSpec(memory_space=pltpu.SMEM if i < scalars else pltpu.VMEM)
        for i in range(len(args))
    ]
    return pl.pallas_call(
        kernel,
        out_shape=[jax.ShapeDtypeStruct(s, d) for s, d in outs],
        in_specs=specs,
        out_specs=[pl.BlockSpec(memory_space=pltpu.VMEM) for _ in outs],
        scratch_shapes=list(scratch),
        compiler_params=pltpu.CompilerParams(vmem_limit_bytes=room(args, outs, scratch)),
        cost_estimate=pl.CostEstimate(flops=flops, bytes_accessed=0, transcendentals=0),
    )(*args)


def spread(x, axis, size):
    return [x] + [
        lax.ppermute(x, axis, [(i, i ^ k) for i in range(size)]) for k in range(1, size)
    ]


def gather_pairs(few, rest, own_pack, nq):
    half = nq // 2
    more = [len(slots) > FEW for slots in stored(nq)]
    mirror = [(i, nq - 1 - i) for i in range(nq)]
    few_in = lax.ppermute(few, "col", mirror)
    rest_in = lax.ppermute(rest, "col", [pair for pair in mirror if more[pair[0]]])
    pack_in = lax.ppermute(own_pack, "col", mirror)
    front = jnp.where(lax.axis_index("col") >= half, few, few_in)
    fronts = tree_gather(front, "col", half, drop_low, 2, levels=1)
    rest_in, fronts = lax.optimization_barrier((rest_in, fronts))
    (back,) = call(
        functools.partial(back_kernel, nq),
        [((TERMS + 2 * PACK - FRONT, BW), f32)],
        (few, rest, few_in, rest_in, own_pack, pack_in),
        0,
    )
    backs = tree_gather(back, "col", half, drop_high, 2)
    fronts = tree_gather(front, "col", half, drop_low, 2, fronts)
    return [got[m] for got in (fronts, backs) for m in range(half)]


def drop_low(m):
    return m & (m - 1)


def drop_high(m):
    return m ^ (1 << (m.bit_length() - 1))


def tree_gather(x, axis, size, parent, repeat=1, got=None, levels=8):
    depth = lambda m: 0 if m == 0 else 1 + depth(parent(m))
    got = dict(got or {0: x})
    for m in sorted(range(1, size), key=lambda m: (depth(m), -m)):
        if m in got or depth(m) > levels:
            continue
        step = m ^ parent(m)
        got[m] = lax.ppermute(got[parent(m)], axis, [(i, i ^ step) for i in range(size * repeat)])
    return got


def along(x, nq):
    return [x] + [
        lax.ppermute(x, "col", [(i, i ^ (2 * k)) for i in range(nq)]) for k in range(1, nq // 2)
    ]


def across(parts, nq):
    joined = jnp.concatenate(parts)
    return parts + [lax.ppermute(joined, "col", [(i, i ^ 1) for i in range(nq)])]


def body(upper_blocks, members):
    nr, nq = lax.axis_size("row"), lax.axis_size("col")
    blocks = upper_blocks[0]
    slots = blocks.shape[0]
    order = nq * BW
    npair = len(pattern(nq))

    few, rest, row_part = call(
        functools.partial(prepare_kernel, nq),
        [((FRONT, BW), f32), (((ALL - FEW) * BW, BW), f32), ((3 * BW + 8, BW), f32)],
        (members, blocks),
        0,
    )
    row = tree_gather(row_part, "row", nr, drop_low)
    row = [row[k] for k in range(nr)]
    lists = jnp.concatenate([x[3 * BW : 3 * BW + 1, :slots] for x in row]).astype(jnp.int32)

    square_flops = 6 * order**3
    listed = (npair, BW, BW)
    dense = (order, order)
    edges = (nr, BW, BW)
    pack = (PACK, BW)
    cross_outs = [(edges, f32)] * 4 + [(pack, f32)]
    square_outs = [(listed, f32), (dense, bf16), (dense, bf16), (pack, f32)]

    d, u, su, v, own = call(
        functools.partial(cross_first_kernel, nr, nq), cross_outs, (lists, *row), 1,
        [pltpu.VMEM((nr, 3 * BW + 8, BW), f32)],
    )
    nears = gather_pairs(few, rest, own, nq)
    m, mh, ml, link, s, sh, sl, tell, packs = call(
        functools.partial(first_kernel, nq),
        [(listed, f32), (dense, bf16), (dense, bf16), ((nq, order), f32)]
        + square_outs
        + [((nq,) + pack, f32)],
        (*nears, own),
        0,
        [pltpu.VMEM((nq // 2, TERMS + 2 * PACK, BW), f32)],
        flops=square_flops,
    )
    packs = [packs]
    rows = spread(tell, "row", nr)
    for step in range(PURIFY - 1):
        x, y = call(
            functools.partial(cube_kernel, nq),
            [(listed, f32)] * 2,
            (m, mh, ml, s, sh, sl, link),
            0,
            flops=square_flops,
        )
        if step == PURIFY - 2:
            break
        coef, d, u, su, v, own = call(
            functools.partial(cross_kernel, nr, nq, len(packs)),
            [((8, BW), f32)] + cross_outs,
            (lists, *rows, *packs, d, u, su, v),
            1,
            [pltpu.VMEM((nq, 8, BW), f32), pltpu.VMEM((nr, PACK, BW), f32)],
            flops=square_flops // 4,
        )
        old = packs
        straight = along(own, nq)
        m, mh, ml, s, sh, sl, tell = call(
            functools.partial(next_kernel, nq, len(old)),
            [(listed, f32), (dense, bf16), (dense, bf16)] + square_outs,
            (coef, *old, own, x, y, m, link),
            0,
            [pltpu.VMEM((nq, PACK, BW), f32)],
            flops=square_flops,
        )
        tell, *straight = lax.optimization_barrier((tell, *straight))
        rows = spread(tell, "row", nr)
        packs = across(straight, nq)
    strip = (order, BW)
    xo, yo, sums = call(
        functools.partial(last_kernel, nr, nq, len(packs)),
        [((slots, BW, BW), f32)] * 2 + [((8, BW), f32)],
        (lists, *rows, *packs, x, y, m, link, d, u, su, v),
        1,
        [
            pltpu.VMEM((nr, PACK, BW), f32),
            pltpu.VMEM((nq, 8, BW), f32),
            pltpu.VMEM((nq, PACK, BW), f32),
            pltpu.VMEM(listed, f32),
            pltpu.VMEM(dense, bf16),
            pltpu.VMEM(dense, bf16),
            pltpu.VMEM(strip, f32),
            pltpu.VMEM(strip, f32),
        ],
    )
    lane = jnp.arange(BW) < BW // 2
    mine = jnp.where(lane, sums[0], sums[1])
    parts = lax.all_to_all(
        jnp.broadcast_to(mine[None], (nr * nq, BW)), ("row", "col"), 0, 0, tiled=True
    )
    (out,) = call(
        functools.partial(finish_kernel, slots),
        [((1, slots, BW, BW), f32)],
        (parts, xo, yo),
        0,
    )
    return out


def solution(mesh):
    return jax.shard_map(
        body,
        mesh=mesh,
        in_specs=(P(("row", "col"), None, None, None), P(("row", "col"), None)),
        out_specs=P(("row", "col"), None, None, None),
        check_vma=False,
    )
```
